256 devices in a mesh: row: 16 (over y, z_hi), col: 16 (over x, z_lo, core).
Axes of the slice: x: 4, y: 4, z: 8 (z_hi: 4, z_lo: 2; z = z_hi * 2 + z_lo), core: 2. Of those that a mesh axis runs over, the one named last changes fastest.
Arguments:
- hidden_in: bfloat16 [1024, 8192], P('col', 'row'), may hold values from -6 to 6
- block_norm_gain: float32 [8192], P('row'), may hold values from 0.5 to 1.5
- query_weight: bfloat16 [8192, 8192], P('row', 'col'), may hold values from -0.0625 to 0.0625
- key_weight: bfloat16 [8192, 1024], P('row', 'col'), may hold values from -0.0625 to 0.0625
- value_weight: bfloat16 [8192, 1024], P('row', 'col'), may hold values from -0.0625 to 0.0625
- out_weight: bfloat16 [8192, 8192], P('row', 'col'), may hold values from -0.0625 to 0.0625
- cotangent: bfloat16 [1024, 8192], P('col', 'row'), may hold values from -6 to 6
- action_mask: int32 [1024], P('col'), may hold values from 0 to 1, as said below
- segment_ids: int32 [1024], replicated, may hold values from 0 to 3, never falling along the last dimension, each value on 1 to 512 neighbouring positions
Outputs:
- residual_input_grad: bfloat16 [1024, 8192], P('col', 'row')
- grad_norm_gain: float32 [8192], P('row')
- grad_query_weight: float32 [8192, 8192], P('row', 'col')
- grad_key_weight: float32 [8192, 1024], P('row', 'col')
- grad_value_weight: float32 [8192, 1024], P('row', 'col')
- grad_out_weight: float32 [8192, 8192], P('row', 'col')
- norm_inner: float32 [1024], P('col')
The draws below stay inside these ranges and needn't reach their ends.
Inputs may be any that keep to these rules, and one draw needn't show every extreme that they name: `action_mask`: the last token of the batch is always an action token. `segment_ids`: episodes are contiguous runs numbered in order.
All inputs are finite; a program needn't handle non-finite values.
Results may differ from the reference program's by a relative error of at most 0.012.
Values may be sent and summed in bfloat16 or wider, within the bound.
No kernel may reach another device: no remote copies, remote signals or barrier semaphores. Data moves between devices by JAX's collectives and lax.ppermute only.
A program may use at most 64 MiB of HBM per device.

```python
import math
import jax
import jax.numpy as jnp
import numpy as np
from jax import lax

MODEL_WIDTH = 8192
HEADS = 64
KV_HEADS = 8
DH = 128
TOKENS = 1024


def draw_action_mask(key, part):
    key = jax.random.fold_in(key, 11)
    chance = jax.random.randint(key, (TOKENS,), 0, 1000)
    place = jnp.arange(TOKENS, dtype=jnp.int32)
    limit = 150 + 450 * place // TOKENS
    marked = jnp.where(chance < limit, 1, 0)
    return jnp.where(place == TOKENS - 1, 1, marked).astype(jnp.int32)


def block_scale(key, dims, pieces, low, top_value):
    level = 1.0
    for position, parts in pieces:
        heights = jax.random.uniform(jax.random.fold_in(jax.random.fold_in(key, 6), position), (parts,), jnp.float32, low / len(pieces), top_value / len(pieces))
        level = level * jnp.repeat(jnp.exp(heights), dims[position] // parts).reshape((-1,) + (1,) * (len(dims) - 1 - position))
    return level


def length_profile(count, total, bound, slope):
    portions = [(1 << 20) // math.isqrt(rank ** slope) + 1 for rank in range(2, count + 1)]
    rest, given = total - bound - (count - 1), [1] * (count - 1)
    while rest > 0:
        free = [i for i in range(count - 1) if given[i] < bound]
        mass, budget = sum([portions[i] for i in free]), rest
        for i in free:
            addition = min(bound - given[i], max(1, budget * portions[i] // mass), rest)
            given[i] = given[i] + addition
            rest = rest - addition
    return np.array([bound] + given)


def uneven_parts(stream_key, amount, total, most, lean):
    if amount == 2:
        one = jax.random.randint(stream_key, (), max(1, total - most), min(most, total - 1) + 1)
        return jnp.stack([one, total - one])
    lengths = jnp.asarray(length_profile(amount, total, most, lean), jnp.int32)
    couples = (amount - 1) // 2
    donor, sink = lengths[1:1 + 2 * couples:2], lengths[2:2 + 2 * couples:2]
    room = jnp.minimum(donor - 1, most - sink)
    moved = jax.random.randint(jax.random.fold_in(stream_key, 1), (couples,), 0, 1 << 20) % (room + 1)
    lengths = lengths.at[1:1 + 2 * couples:2].set(donor - moved).at[2:2 + 2 * couples:2].set(sink + moved)
    return lengths[jax.random.permutation(jax.random.fold_in(stream_key, 2), amount)]


def centred(rng, extent, scale, most, cuts=(), held_as=jnp.bfloat16):
    entries = scale * jax.random.normal(rng, extent, jnp.float32)
    if cuts:
        entries = entries * block_scale(rng, extent, cuts, -0.22, 0.18)
    return jnp.clip(entries, -most, most).astype(held_as)


def setup_inputs(seed: int = 0) -> dict:
    arg_keys = jax.random.split(jax.random.key(seed), 10)
    hidden_in = centred(arg_keys[0], (TOKENS, MODEL_WIDTH), 1.0, 6.0, ((0, 16), (1, 16)))
    block_norm_gain = jnp.clip(1.0 + 0.1 * jax.random.normal(arg_keys[1], (MODEL_WIDTH,), jnp.float32), 0.5, 1.5)
    query_weight = centred(arg_keys[2], (MODEL_WIDTH, HEADS * DH), MODEL_WIDTH ** -0.5, 0.0625, ((0, 16), (1, 16)))
    key_weight = centred(arg_keys[3], (MODEL_WIDTH, KV_HEADS * DH), MODEL_WIDTH ** -0.5, 0.0625, ((0, 16), (1, 16)))
    value_weight = centred(arg_keys[4], (MODEL_WIDTH, KV_HEADS * DH), MODEL_WIDTH ** -0.5, 0.0625, ((0, 16), (1, 16)))
    out_weight = centred(arg_keys[5], (MODEL_WIDTH, HEADS * DH), (HEADS * DH) ** -0.5, 0.0625, ((0, 16), (1, 16)))
    cotangent = centred(arg_keys[6], (TOKENS, MODEL_WIDTH), 1.0, 6.0, ((0, 16), (1, 16)))
    action_mask = draw_action_mask(jax.random.fold_in(arg_keys[9], 71), 0)
    segment_ids = jnp.searchsorted(jnp.cumsum(uneven_parts(arg_keys[8], 4, TOKENS, TOKENS // 2, 0)), jnp.arange(TOKENS), side="right").astype(jnp.int32)
    return dict(hidden_in=hidden_in, block_norm_gain=block_norm_gain, query_weight=query_weight, key_weight=key_weight, value_weight=value_weight, out_weight=out_weight, cotangent=cotangent, action_mask=action_mask, segment_ids=segment_ids)


rope_theta = 500000.0
norm_eps = 1e-05

def rotate(values, positions, first_col, head_dim, direction):
    column = first_col + jnp.arange(values.shape[1], dtype=jnp.int32)
    within = column % head_dim
    pair_rate = jnp.exp((within // 2).astype(jnp.float32) * (-2.0 * math.log(rope_theta) / head_dim))
    angle = positions.astype(jnp.float32)[:, None] * pair_rate[None, :]
    is_even = (within % 2 == 0)[None, :]
    swapped = jnp.where(is_even, jnp.roll(values, -1, axis=1), jnp.roll(values, 1, axis=1))
    signed = jnp.where(is_even, -jnp.sin(angle), jnp.sin(angle)) * direction
    return values * jnp.cos(angle) + swapped * signed

def settle(values):
    return lax.optimization_barrier(values.astype(jnp.bfloat16)).astype(jnp.float32)

def reference(hidden_in, block_norm_gain, query_weight, key_weight, value_weight, out_weight, cotangent, action_mask, segment_ids):
    residual_float = hidden_in.astype(jnp.float32)
    inverse_deviation = lax.rsqrt(lax.optimization_barrier(jnp.sum(residual_float * residual_float, axis=1)) / MODEL_WIDTH + norm_eps)
    standardized_input = residual_float * inverse_deviation[:, None]
    normalized_input = lax.optimization_barrier((standardized_input * block_norm_gain[None, :]).astype(jnp.bfloat16))
    weights_all = jnp.concatenate([query_weight, key_weight, value_weight], axis=1)
    proj = jnp.dot(normalized_input, weights_all, preferred_element_type=jnp.float32)
    qcols = HEADS * DH
    kcols = KV_HEADS * DH
    positions = jnp.arange(TOKENS, dtype=jnp.int32)
    queries = lax.optimization_barrier(rotate(proj[:, :qcols], positions, 0, DH, 1.0).astype(jnp.bfloat16))
    keys_all = lax.optimization_barrier(rotate(proj[:, qcols:qcols + kcols], positions, 0, DH, 1.0).astype(jnp.bfloat16))
    values_all = lax.optimization_barrier(proj[:, qcols + kcols:].astype(jnp.bfloat16))
    mask_f = action_mask.astype(jnp.float32)
    count = jnp.sum(mask_f)
    gain_scaled_grad = lax.optimization_barrier((cotangent.astype(jnp.float32) * (mask_f * (TOKENS / count))[:, None]).astype(jnp.bfloat16))
    d_attended = lax.optimization_barrier(jnp.dot(gain_scaled_grad, out_weight, preferred_element_type=jnp.float32).astype(jnp.bfloat16))
    allowed = (segment_ids[:, None] == segment_ids[None, :]) & (positions[None, :] <= positions[:, None])
    group = HEADS // KV_HEADS
    span = group * DH
    scale = DH ** (-0.5)

    def one_head(kv_head):
        qg = lax.dynamic_slice_in_dim(queries, kv_head * span, span, 1).astype(jnp.float32).reshape(TOKENS, group, DH)
        keys_h = lax.dynamic_slice_in_dim(keys_all, kv_head * DH, DH, 1).astype(jnp.float32)
        values_h = lax.dynamic_slice_in_dim(values_all, kv_head * DH, DH, 1).astype(jnp.float32)
        grad_o = lax.dynamic_slice_in_dim(d_attended, kv_head * span, span, 1).astype(jnp.float32).reshape(TOKENS, group, DH)
        scores = jnp.einsum('tgd,ud->gtu', qg, keys_h) * scale
        scores = jnp.where(allowed[None], scores, -jnp.inf)
        top = lax.optimization_barrier(jnp.max(scores, axis=-1, keepdims=True))
        total_e = lax.optimization_barrier(jnp.sum(jnp.exp(scores - top), axis=-1, keepdims=True))
        probs = jnp.exp(scores - (top + jnp.log(total_e)))
        probs_b = settle(probs)
        attended = lax.optimization_barrier(jnp.einsum('gtu,ud->tgd', probs_b, values_h).astype(jnp.bfloat16))
        delta = jnp.transpose(lax.optimization_barrier(jnp.sum(grad_o * attended.astype(jnp.float32), axis=-1)), (1, 0))[:, :, None]
        dprobs = jnp.einsum('tgd,ud->gtu', grad_o, values_h)
        dscores = settle(probs * (dprobs - delta))
        dq_raw = jnp.einsum('gtu,ud->tgd', dscores, keys_h) * scale
        dk_raw = jnp.einsum('gtu,tgd->ud', dscores, qg) * scale
        dv_raw = jnp.einsum('gtu,tgd->ud', probs_b, grad_o)
        return (attended.reshape(TOKENS, span), dq_raw.reshape(TOKENS, span), dk_raw, dv_raw)
    stacked = lax.map(one_head, jnp.arange(KV_HEADS, dtype=jnp.int32))
    attended_all = jnp.transpose(stacked[0], (1, 0, 2)).reshape(TOKENS, qcols)
    dq_all = jnp.transpose(stacked[1], (1, 0, 2)).reshape(TOKENS, qcols)
    dk_all = jnp.transpose(stacked[2], (1, 0, 2)).reshape(TOKENS, kcols)
    dv_all = jnp.transpose(stacked[3], (1, 0, 2)).reshape(TOKENS, kcols)
    dq_b = rotate(dq_all, positions, 0, DH, -1.0).astype(jnp.bfloat16)
    dk_b = rotate(dk_all, positions, 0, DH, -1.0).astype(jnp.bfloat16)
    dv_b = dv_all.astype(jnp.bfloat16)
    d_proj = jnp.concatenate([dq_b, dk_b, dv_b], axis=1)
    grad_all = jnp.dot(normalized_input.T, d_proj, preferred_element_type=jnp.float32)
    grad_out_weight = jnp.dot(gain_scaled_grad.T, attended_all, preferred_element_type=jnp.float32)
    normalized_output_grad = jnp.dot(d_proj, weights_all.T, preferred_element_type=jnp.float32)
    gain_gradient_total = lax.optimization_barrier(jnp.sum(normalized_output_grad * standardized_input, axis=0))
    centered_grad = normalized_output_grad * block_norm_gain[None, :]
    norm_inner = lax.optimization_barrier(jnp.sum(centered_grad * standardized_input, axis=1))
    mean_correction = norm_inner / MODEL_WIDTH
    residual_input_grad = (gain_scaled_grad.astype(jnp.float32) + inverse_deviation[:, None] * (centered_grad - standardized_input * mean_correction[:, None])).astype(jnp.bfloat16)
    return (residual_input_grad, gain_gradient_total, grad_all[:, :qcols], grad_all[:, qcols:qcols + kcols], grad_all[:, qcols + kcols:], grad_out_weight, norm_inner)
```

```python
import math

import jax
import jax.numpy as jnp
from jax import lax
from jax.experimental import pallas as pl
from jax.experimental.pallas import tpu as pltpu
from jax.sharding import PartitionSpec as P

DH = 128
WIDTH = 8192
TOKENS = 1024
rope_theta = 500000.0
norm_eps = 1e-05
F32 = jnp.float32
BF16 = jnp.bfloat16

STEPS = {
    "y": ("row", lambda i, k: (i // 4 + k) % 4 * 4 + i % 4),
    "zh": ("row", lambda i, k: i // 4 * 4 + (i % 4 + k) % 4),
    "x": ("col", lambda i, k: (i // 4 + k) % 4 * 4 + i % 4),
    "zl": ("col", lambda i, k: i ^ 2),
    "c": ("col", lambda i, k: i ^ 1),
}


def shift(array, axis, k=1):
    name, place = STEPS[axis]
    return lax.ppermute(array, name, [(i, place(i, k)) for i in range(16)])


def spread(arrays, axis, sign=1):
    got = {k: shift(arrays[k], axis, (sign * k) % 4) for k in (1, 3, 2)}
    return [got[1], got[2], got[3]]


def call(body, outs, *args, scratch=()):
    specs = [
        pl.BlockSpec(memory_space=pltpu.SMEM if a.dtype == jnp.int32 else pltpu.VMEM) for a in args
    ]
    return pl.pallas_call(
        body,
        out_shape=[jax.ShapeDtypeStruct(s, d) for s, d in outs],
        in_specs=specs,
        out_specs=[pl.BlockSpec(memory_space=pltpu.VMEM)] * len(outs),
        scratch_shapes=list(scratch),
        compiler_params=pltpu.CompilerParams(vmem_limit_bytes=40 * 1024 * 1024),
    )(*args)


def dot(a, b, ca=1, cb=0):
    return lax.dot_general(a, b, (((ca,), (cb,)), ((), ())), preferred_element_type=F32)


def at(base, size):
    return pl.ds(pl.multiple_of(base, size), size)


def halves(row):
    hi = row.astype(BF16).astype(F32)
    return hi, row - hi


def stat_rows(rows, lanes):
    place = lax.broadcasted_iota(jnp.int32, (16, lanes), 0)
    out = jnp.zeros((16, lanes), F32)
    for i, row in enumerate(rows):
        hi, lo = halves(row)
        out = jnp.where(place == 2 * i, hi, out)
        out = jnp.where(place == 2 * i + 1, lo, out)
    return out.astype(BF16)


def read_stat(ref, start, count):
    block = ref[start : start + 16, :].astype(F32)
    return [block[2 * i : 2 * i + 1] + block[2 * i + 1 : 2 * i + 2] for i in range(count)]


def lane_sums(values):
    part = values[:, :128]
    for j in range(1, values.shape[1] // 128):
        part = part + values[:, j * 128 : (j + 1) * 128]
    return [
        jnp.sum(part[i * 128 : (i + 1) * 128].T, axis=0, keepdims=True)
        for i in range(values.shape[0] // 128)
    ]


def columns(rows):
    return jnp.concatenate([jnp.broadcast_to(r, (128, 128)).T for r in rows], axis=0)


def swap_pairs(v):
    even = lax.broadcasted_iota(jnp.int32, v.shape, 1) % 2 == 0
    return jnp.where(even, pltpu.roll(v, 127, 1), pltpu.roll(v, 1, 1))


def k_norm_kv(idx, mine, other, gain, wkv, x_full, xg_full, m0, m1, m2, m3):
    y, c = idx[0], idx[4]
    x_full[at(c * 512, 512), :] = mine[...]
    x_full[at((1 - c) * 512, 512), :] = other[...]
    for k, out in enumerate((m0, m1, m2, m3)):
        rows = at(lax.rem(y + k, 4) * 256, 256)
        xf = x_full[rows, :].astype(F32)
        xg = (xf * gain[...]).astype(BF16)
        xg_full[rows, :] = xg
        out[0:256, :] = dot(xg, wkv[...]).astype(BF16)
        out[256:272, :] = stat_rows(lane_sums(xf * xf), 128)


def k_mm_y(idx, xg_full, w, m0, m1, m2, m3):
    y = idx[0]
    for k, out in enumerate((m0, m1, m2, m3)):
        out[...] = dot(xg_full[at(lax.rem(y + k, 4) * 256, 256), :], w[...]).astype(BF16)


def k_ct(idx, mine, other, w, full, m0, m1, m2, m3, cscale):
    y, c = idx[0], idx[4]
    count = jnp.zeros((16, 512), F32)
    for ref, base in ((mine, c * 512), (other, (1 - c) * 512)):
        for j in range(8):
            full[at(base + j * 64, 64), :] = ref[j * 80 : j * 80 + 64, :]
            count = count + ref[j * 80 + 64 : j * 80 + 80, :].astype(F32)
    cscale[...] = TOKENS / count[0:8, 0:128]
    k_mm_y(idx, full, w, m0, m1, m2, m3)


def k_sum_heads(idx, a, b, c, d, m0, m1, m2, m3):
    zh = idx[1]
    for k, out in enumerate((m0, m1, m2, m3)):
        lanes = at(lax.rem(zh + k, 4) * 128, 128)
        out[...] = sum(r[:, lanes].astype(F32) for r in (a, b, c, d)).astype(BF16)


def k_sum_kv(a, b, c, d, out):
    out[0:256, :] = sum(r[0:256, :].astype(F32) for r in (a, b, c, d)).astype(BF16)
    stats = [read_stat(r, 256, 2) for r in (a, b, c, d)]
    out[256:272, :] = stat_rows([sum(s[i] for s in stats) for i in range(2)], 128)


def k_kv(a, b, c, d, cos, sin, kv, proj, rstd):
    stats = [read_stat(r, 256, 2) for r in (a, b, c, d)]
    rows = [lax.rsqrt(sum(s[i] for s in stats) / WIDTH + norm_eps) for i in range(2)]
    scale = columns(rows)
    p = sum(r[0:256, :].astype(F32) for r in (a, b, c, d))
    proj[...] = p
    rstd[...] = scale
    v = p * scale
    kv[...] = (v * cos[...] + swap_pairs(v) * sin[...]).astype(BF16)


def token_of(idx, place):
    x = (idx[2] - (place // 128) % 4) & 3
    zl = idx[3] ^ ((place // 64) & 1)
    return x * 256 + zl * 128 + (place // 512) * 64 + (place & 63)


def k_attend(
    idx, q0, q1, q2, q3, d0, d1, d2, d3, cscale, rstd, cos, sin, kvm, kvo, eq, att, keep, send
):
    scale = DH ** (-0.5)
    y, c = idx[0], idx[4]
    proj = sum(r[...].astype(F32) for r in (q0, q1, q2, q3))
    qv = proj * rstd[...]
    q = (qv * cos[...] + swap_pairs(qv) * sin[...]).astype(BF16)
    grad = (sum(r[...].astype(F32) for r in (d0, d1, d2, d3)) * cscale[0:1, :]).astype(BF16)
    mine, other = kvm[...].astype(F32), kvo[...].astype(F32)
    first = c == 0
    lo, hi = jnp.where(first, mine, other), jnp.where(first, other, mine)
    left = lax.broadcasted_iota(jnp.int32, (TOKENS, 128), 1) < 64
    keys = jnp.where(left, lo, pltpu.roll(hi, 64, 1)).astype(BF16)
    values = jnp.where(left, pltpu.roll(lo, 64, 1), hi).astype(BF16)
    t_place = lax.broadcasted_iota(jnp.int32, (256, 1), 0) + y * 256
    t = token_of(idx, t_place)
    start = jnp.zeros((256, 1), jnp.int32)
    for s in range(5, 8):
        start = jnp.where(t >= idx[s], jnp.maximum(start, idx[s]), start)
    u_place = lax.broadcasted_iota(jnp.int32, (1, TOKENS), 1)
    u_place = ((y - u_place // 256) & 3) * 256 + (u_place & 255)
    u = token_of(idx, u_place)
    allowed = (u <= t) & (u >= start)
    scores = jnp.where(allowed, dot(q, keys, 1, 1) * scale, -jnp.inf)
    top = jnp.max(scores, axis=1, keepdims=True)
    e = jnp.exp(scores - top)
    probs = e * (1.0 / jnp.sum(e, axis=1, keepdims=True))
    pb = probs.astype(BF16)
    attended = dot(pb, values).astype(BF16)
    att[...] = attended
    delta = jnp.sum(grad.astype(F32) * attended.astype(F32), axis=1, keepdims=True)
    ds = (probs * (dot(grad, values, 1, 1) - delta)).astype(BF16)
    dq = dot(ds, keys) * scale
    e_q = ((dq * cos[...] - swap_pairs(dq) * sin[...]) * rstd[...]).astype(BF16)
    eq[0:256, :] = e_q
    eq[256:272, :] = stat_rows(lane_sums(e_q.astype(F32) * proj), 128)
    dk = dot(ds, q, 0, 0) * scale
    dv = dot(pb, grad, 0, 0)
    g_lo = jnp.where(left, dk, pltpu.roll(dv, 64, 1))
    g_hi = jnp.where(left, pltpu.roll(dk, 64, 1), dv)
    keep[...] = jnp.where(first, g_lo, g_hi)
    send[...] = jnp.where(first, g_hi, g_lo).astype(BF16)


def k_dkv_core(keep, got, m0, m1, m2, m3):
    for k, out in enumerate((m0, m1, m2, m3)):
        rows = slice(k * 256, (k + 1) * 256)
        out[...] = (keep[rows, :] + got[rows, :].astype(F32)).astype(BF16)


def k_sum4(a, b, c, d, out):
    out[...] = sum(r[...].astype(F32) for r in (a, b, c, d)).astype(BF16)


def k_dkv(a, b, c, d, cos, sin, rstd, proj, out):
    g = sum(r[...].astype(F32) for r in (a, b, c, d))
    e = ((g * cos[...] - swap_pairs(g) * sin[...]) * rstd[...]).astype(BF16)
    out[0:256, :] = e
    rows = lane_sums(e.astype(F32) * proj[...])
    scales = [rstd[i * 128 : (i + 1) * 128, :].T[0:1, :] for i in range(2)]
    out[256:272, :] = stat_rows(rows + scales, 128)


def k_pack_heads(idx, a, b, c, d, out):
    zh = idx[1]
    refs = (a, b, c, d)
    for k, r in enumerate(refs):
        out[0:256, at(((zh - k) & 3) * 128, 128)] = r[0:256, :]
    stats = [read_stat(r, 256, 2) for r in refs]
    block = stat_rows([sum(s[i] for s in stats) for i in range(2)], 128)
    for k in range(4):
        out[256:272, k * 128 : (k + 1) * 128] = block


def k_pack_att(idx, a, b, c, d, out):
    zh = idx[1]
    for k, r in enumerate((a, b, c, d)):
        out[:, at(((zh - k) & 3) * 128, 128)] = r[...]


def k_dnorm(
    idx, q0, q1, q2, q3, k0, k1, k2, k3, wq, wkv, x_full, send, keep, keep_stat, rstd, grad, nsum, rsum
):
    y, c = idx[0], idx[4]
    gain = jnp.zeros((1, 512), F32)
    for k, (q, kv) in enumerate(((q0, k0), (q1, k1), (q2, k2), (q3, k3))):
        block = (y - k) & 3
        rows = at(block * 256, 256)
        g = dot(q[0:256, :], wq[...], 1, 1) + dot(kv[0:256, :], wkv[...], 1, 1)
        grad[rows, :] = g
        gain = gain + jnp.sum(g * x_full[rows, :].astype(F32), axis=0, keepdims=True)
        nq = read_stat(q, 256, 2)
        nk = read_stat(kv, 256, 4)
        for i in range(2):
            lanes = slice(i * 128, (i + 1) * 128)
            nsum[block, :, lanes] = jnp.broadcast_to(nq[i][:, :128] + nk[i], (8, 128))
            rsum[block, :, lanes] = jnp.broadcast_to(nk[2 + i], (8, 128))
    n = [jnp.concatenate([nsum[2 * h, 0:1, :], nsum[2 * h + 1, 0:1, :]], axis=1) for h in (c, 1 - c)]
    there = at((1 - c) * 512, 512)
    here = at(c * 512, 512)
    send[0:512, :] = grad[there, :].astype(BF16)
    send[512:528, :] = stat_rows([gain, n[1]], 512)
    keep[...] = grad[here, :]
    keep_stat[0:1, :] = gain
    keep_stat[1:2, :] = n[0]
    rstd[...] = rsum[2 * c, :, 0:128]


def k_g_core(keep, keep_stat, got, m0, m1, m2, m3):
    gain, n = read_stat(got, 512, 2)
    gain = gain + keep_stat[0:1, :]
    n = n + keep_stat[1:2, :]
    for k, out in enumerate((m0, m1, m2, m3)):
        rows = slice(k * 128, (k + 1) * 128)
        out[0:128, :] = (keep[rows, :] + got[rows, :].astype(F32)).astype(BF16)
        part = jnp.concatenate([n[:, k * 128 : (k + 1) * 128], jnp.zeros((1, 384), F32)], axis=1)
        out[128:144, :] = stat_rows([gain, part], 512)


def k_g_x(a, b, c, d, keep, send):
    refs = (a, b, c, d)
    stats = [read_stat(r, 128, 2) for r in refs]
    gain, n = (sum(s[i] for s in stats) for i in range(2))
    total = sum(r[0:128, :].astype(F32) for r in refs)
    keep[0:64, :] = total[0:64]
    keep[64:65, :] = gain
    keep[65:66, :] = n
    send[0:64, :] = total[64:128].astype(BF16)
    n_there = jnp.concatenate([n[:, 64:128], n[:, 0:64], n[:, 128:512]], axis=1)
    send[64:80, :] = stat_rows([gain, n_there], 512)


def k_final(keep, got, x, ct, gain_in, cscale, rstd, res, gain, inner):
    stats = read_stat(got, 64, 2)
    gain[...] = keep[64:65, :] + stats[0]
    n = (keep[65:66, :] + stats[1])[:, 0:128]
    inner[...] = n
    scale = rstd[0:1, :]
    corr = columns([scale * scale * n * (1.0 / WIDTH)])[0:64]
    g = keep[0:64, :] + got[0:64, :].astype(F32)
    for j in range(4):
        lanes = slice(j * 128, (j + 1) * 128)
        scaled = (ct[:, lanes].astype(F32) * cscale[0:1, :]).astype(BF16).astype(F32)
        res[:, lanes] = (
            scaled + g[:, lanes] * gain_in[:, lanes] - x[:, lanes].astype(F32) * corr
        ).astype(BF16)


def k_grad_w(idx, xg_full, q0, q1, q2, q3, k0, k1, k2, k3, gq, gk, gv):
    y = idx[0]
    gkv = jnp.zeros((512, 128), F32)
    for k, (q, kv) in enumerate(((q0, k0), (q1, k1), (q2, k2), (q3, k3))):
        left = xg_full[at(((y - k) & 3) * 256, 256), :].T
        part = dot(left, q[0:256, :])
        gq[...] = part if k == 0 else gq[...] + part
        gkv = gkv + dot(left, kv[0:256, :])
    gk[...] = gkv[:, 0:64]
    gv[...] = gkv[:, 64:128]


def k_grad_o(idx, ct_full, a, b, c, d, cscale, go):
    y = idx[0]
    for k, r in enumerate((a, b, c, d)):
        part = dot(ct_full[at(((y - k) & 3) * 256, 256), :].T, r[...])
        go[...] = part if k == 0 else go[...] + part
    go[...] = go[...] * cscale[0:1, 0:1]


def rope_tables(tok, column, width):
    rate = jnp.exp((column // 2).astype(F32) * (-2.0 * math.log(rope_theta) / DH))
    angle = tok.astype(F32)[:, None] * rate[None, :]
    turned = (jnp.arange(128) < width)[None, :]
    even = (jnp.arange(128) % 2 == 0)[None, :]
    sin = jnp.sin(angle)
    return jnp.where(turned, jnp.cos(angle), 1.0), jnp.where(turned, jnp.where(even, -sin, sin), 0.0)


def shards(hidden, gain, wq, wk, wv, wo, cotangent, mask, segments):
    row, col = lax.axis_index("row"), lax.axis_index("col")
    y, zh, x, zl, c = row // 4, row % 4, col // 4, col // 2 % 2, col % 2
    starts = [jnp.sum((segments < s).astype(jnp.int32)) for s in (1, 2, 3)]
    idx = jnp.stack([y, zh, x, zl, c, *starts]).astype(jnp.int32)
    gain2 = gain[None, :]
    wkv = jnp.concatenate([wk, wv], axis=1)
    big = ((256, 512), BF16)

    xs = jnp.concatenate([hidden, shift(hidden, "zl")], axis=0)
    x_mine = jnp.concatenate([xs, *spread([xs] * 4, "x")], axis=0)
    x_other = shift(x_mine, "c")

    ctm = jnp.where((mask > 0)[:, None], cotangent, jnp.zeros_like(cotangent))
    number = jnp.broadcast_to(jnp.sum(mask.astype(F32)), (16, 512)).astype(BF16)
    ct0 = jnp.concatenate([ctm, number], axis=0)
    cs = jnp.concatenate([ct0, shift(ct0, "zl")], axis=0)
    ct_mine = jnp.concatenate([cs, *spread([cs] * 4, "x")], axis=0)
    ct_other = shift(ct_mine, "c")

    tok = token_of(idx, y * 256 + jnp.arange(256, dtype=jnp.int32))
    cos_q, sin_q = rope_tables(tok, jnp.arange(128, dtype=jnp.int32), 128)
    cos_k, sin_k = rope_tables(tok, (c * 64 + jnp.arange(128, dtype=jnp.int32)) % 128, 64)

    x_full, xg_full, *kv_part = call(
        k_norm_kv,
        [((1024, 512), BF16)] * 2 + [((272, 128), BF16)] * 4,
        idx, x_mine, x_other, gain2, wkv,
    )
    kv_got = spread(kv_part, "y")
    q_part = call(k_mm_y, [big] * 4, idx, xg_full, wq)
    q_got = spread(q_part, "y")
    (kv_sum,) = call(k_sum_kv, [((272, 128), BF16)], kv_part[0], *kv_got)
    kv_all = spread([kv_sum] * 4, "zh")
    ct_full, d0, d1, d2, d3, cscale = call(
        k_ct, [((1024, 512), BF16)] + [big] * 4 + [((8, 128), F32)], idx, ct_mine, ct_other, wo
    )
    d_got = spread([d0, d1, d2, d3], "y")
    q_heads = call(k_sum_heads, [((256, 128), BF16)] * 4, idx, q_part[0], *q_got)
    q_all = spread(q_heads, "zh")
    kv, proj_kv, rstd = call(
        k_kv,
        [((256, 128), BF16), ((256, 128), F32), ((256, 128), F32)],
        kv_sum, *kv_all, cos_k, sin_k,
    )
    kv_mine = jnp.concatenate([kv, *spread([kv] * 4, "y")], axis=0)
    kv_other = shift(kv_mine, "c")
    d_heads = call(k_sum_heads, [((256, 128), BF16)] * 4, idx, d0, *d_got)
    d_all = spread(d_heads, "zh")

    eq, att, keep, send = call(
        k_attend,
        [((272, 128), BF16), ((256, 128), BF16), ((1024, 128), F32), ((1024, 128), BF16)],
        idx, q_heads[0], *q_all, d_heads[0], *d_all, cscale, rstd, cos_q, sin_q, kv_mine, kv_other,
    )
    dkv = call(k_dkv_core, [((256, 128), BF16)] * 4, keep, shift(send, "c"))
    dkv_got = spread(dkv, "y", -1)
    eq_all = spread([eq] * 4, "zh")
    (dkv_sum,) = call(k_sum4, [((256, 128), BF16)], dkv[0], *dkv_got)
    dkv_all = spread([dkv_sum] * 4, "zh")
    (eq_row,) = call(k_pack_heads, [((272, 512), BF16)], idx, eq, *eq_all)
    eq_rows = [eq_row, *spread([eq_row] * 4, "y")]
    (ekv,) = call(
        k_dkv, [((272, 128), BF16)], dkv_sum, *dkv_all, cos_k, sin_k, rstd, proj_kv
    )
    ekv_rows = [ekv, *spread([ekv] * 4, "y")]

    send_g, keep_g, keep_stat, rstd_col = call(
        k_dnorm,
        [((528, 512), BF16), ((512, 512), F32), ((8, 512), F32), ((8, 128), F32)],
        idx, *eq_rows, *ekv_rows, wq, wkv, x_full,
        scratch=[pltpu.VMEM((1024, 512), F32), pltpu.VMEM((4, 8, 256), F32), pltpu.VMEM((4, 8, 256), F32)],
    )
    got_g = shift(send_g, "c")
    g_parts = call(k_g_core, [((144, 512), BF16)] * 4, keep_g, keep_stat, got_g)
    g_got = spread(g_parts, "x", -1)

    att_all = spread([att] * 4, "zh")
    (att_row,) = call(k_pack_att, [((256, 512), BF16)], idx, att, *att_all)
    att_rows = [att_row, *spread([att_row] * 4, "y")]
    gq, gk, gv = call(
        k_grad_w,
        [((512, 512), F32), ((512, 64), F32), ((512, 64), F32)],
        idx, xg_full, *eq_rows, *ekv_rows,
    )
    keep_z, send_z = call(
        k_g_x, [((72, 512), F32), ((80, 512), BF16)], g_parts[0], *g_got
    )
    got_z = shift(send_z, "zl")
    (go,) = call(k_grad_o, [((512, 512), F32)], idx, ct_full, *att_rows, cscale)
    res, gain_grad, inner = call(
        k_final,
        [((64, 512), BF16), ((1, 512), F32), ((1, 128), F32)],
        keep_z, got_z, hidden, ctm, gain2, cscale, rstd_col,
    )
    return res, gain_grad[0], gq, gk, gv, go, inner[0, :64]


def solution(mesh):
    return jax.shard_map(
        shards,
        mesh=mesh,
        in_specs=(
            P("col", "row"),
            P("row"),
            P("row", "col"),
            P("row", "col"),
            P("row", "col"),
            P("row", "col"),
            P("col", "row"),
            P("col"),
            P(),
        ),
        out_specs=(
            P("col", "row"),
            P("row"),
            P("row", "col"),
            P("row", "col"),
            P("row", "col"),
            P("row", "col"),
            P("col"),
        ),
        check_vma=False,
    )
```

```python
import math

import jax
import jax.numpy as jnp
from jax import lax
from jax.experimental import pallas as pl
from jax.experimental.pallas import tpu as pltpu
from jax.sharding import PartitionSpec as P

DH = 128
WIDTH = 8192
TOKENS = 1024
rope_theta = 500000.0
norm_eps = 1e-05
F32 = jnp.float32
BF16 = jnp.bfloat16

STEPS = {
    "y": ("row", lambda i, k: (i // 4 + k) % 4 * 4 + i % 4),
    "zh": ("row", lambda i, k: i // 4 * 4 + (i % 4 + k) % 4),
    "x": ("col", lambda i, k: (i // 4 + k) % 4 * 4 + i % 4),
    "zl": ("col", lambda i, k: i ^ 2),
    "c": ("col", lambda i, k: i ^ 1),
}


def shift(array, axis, k=1):
    name, place = STEPS[axis]
    return lax.ppermute(array, name, [(i, place(i, k)) for i in range(16)])


def spread(arrays, axis, sign=1):
    got = {k: shift(arrays[k], axis, (sign * k) % 4) for k in (1, 3, 2)}
    return [got[1], got[2], got[3]]


def pair(array, axis, k):
    name, _ = STEPS[axis]
    low = 1 if axis == "zh" else 4
    return lax.ppermute(array, name, [(i, i ^ (k * low)) for i in range(16)])


def call(body, outs, *args, scratch=(), unread=()):
    def whole(*refs):
        body(*refs[: len(args)], *refs[len(args) + len(unread) :])

    return pl.pallas_call(
        whole,
        out_shape=[jax.ShapeDtypeStruct(s, d) for s, d in outs],
        in_specs=[pl.BlockSpec(memory_space=pltpu.VMEM)] * len(args)
        + [pl.BlockSpec(memory_space=pl.ANY)] * len(unread),
        out_specs=[pl.BlockSpec(memory_space=pltpu.VMEM)] * len(outs),
        scratch_shapes=list(scratch),
        compiler_params=pltpu.CompilerParams(vmem_limit_bytes=40 * 1024 * 1024),
        name=body.__name__,
    )(*args, *unread)


class Order:
    def __init__(self):
        self.kept = []

    def after(self, value, *others):
        value, *others = lax.optimization_barrier((value, *others))
        self.kept += others
        return value

    def take(self):
        kept, self.kept = self.kept, []
        return kept


def place():
    row, col = lax.axis_index("row"), lax.axis_index("col")
    return row // 4, row % 4, col // 4, col // 2 % 2, col % 2


def dot(a, b, ca=1, cb=0):
    return lax.dot_general(a, b, (((ca,), (cb,)), ((), ())), preferred_element_type=F32)


def at(base, size):
    return pl.ds(pl.multiple_of(base, size), size)


def halves(row):
    hi = row.astype(BF16).astype(F32)
    return hi, row - hi


def stat_rows(rows, lanes):
    place = lax.broadcasted_iota(jnp.int32, (16, lanes), 0)
    out = jnp.zeros((16, lanes), F32)
    for i, row in enumerate(rows):
        hi, lo = halves(row)
        out = jnp.where(place == 2 * i, hi, out)
        out = jnp.where(place == 2 * i + 1, lo, out)
    return out.astype(BF16)


def read_stat(ref, start, count, lane=0):
    block = ref[start : start + 16, lane:].astype(F32)
    return [block[2 * i : 2 * i + 1] + block[2 * i + 1 : 2 * i + 2] for i in range(count)]


def lane_sums(values):
    part = values[:, :128]
    for j in range(1, values.shape[1] // 128):
        part = part + values[:, j * 128 : (j + 1) * 128]
    return [
        jnp.sum(part[i * 128 : (i + 1) * 128].T, axis=0, keepdims=True)
        for i in range(values.shape[0] // 128)
    ]


def columns(rows):
    return jnp.concatenate([jnp.broadcast_to(r, (128, 128)).T for r in rows], axis=0)


def swap_pairs(v):
    even = lax.broadcasted_iota(jnp.int32, v.shape, 1) % 2 == 0
    return jnp.where(even, pltpu.roll(v, 127, 1), pltpu.roll(v, 1, 1))


def token_of(x, zl, spot):
    there = (x - (spot // 128) % 4) & 3
    return there * 256 + (zl ^ ((spot // 64) & 1)) * 128 + (spot // 512) * 64 + (spot & 63)


def k_prep(cotangent, mask, wk, wv, ct, wkv, cos, sin, cos_k, sin_k):
    y, _, x, zl, c = place()
    m = mask[...].astype(F32)
    column = jnp.broadcast_to(jnp.concatenate([m, m], axis=1), (128, 128)).T[0:64]
    for j in range(4):
        lanes = slice(j * 128, (j + 1) * 128)
        ct[0:64, lanes] = jnp.where(column > 0, cotangent[:, lanes].astype(F32), 0.0).astype(BF16)
    count = jnp.sum(m, axis=1, keepdims=True)
    ct[64:80, :] = jnp.broadcast_to(count, (16, 512)).astype(BF16)
    wkv[0:64, :] = wk[...]
    wkv[64:128, :] = wv[...]
    lane = lax.broadcasted_iota(jnp.int32, (1, 128), 1)
    rate = jnp.exp((lane // 2).astype(F32) * (-2.0 * math.log(rope_theta) / DH))
    spot = lax.broadcasted_iota(jnp.int32, (256, 1), 0) + y * 256
    angle = token_of(x, zl, spot).astype(F32) * rate
    co, si = jnp.cos(angle), jnp.sin(angle)
    si = jnp.where(lane % 2 == 0, -si, si)
    cos[...] = co
    sin[...] = si
    cos_k[...] = jnp.where(lane < 64, jnp.where(c == 0, co, pltpu.roll(co, 64, 1)), 1.0)
    sin_k[...] = jnp.where(lane < 64, jnp.where(c == 0, si, pltpu.roll(si, 64, 1)), 0.0)


def k_proj(mine, other, gain, wq, wkv, x_full, xg_full, own, m1, m2, m3):
    y, _, _, _, c = place()
    x_full[at(c * 512, 512), :] = mine[...]
    x_full[at((1 - c) * 512, 512), :] = other[...]
    for k, out in enumerate((own, m1, m2, m3)):
        rows = at(((y + k) & 3) * 256, 256)
        xf = x_full[rows, :].astype(F32)
        xg, rest = split(xf * gain[...])
        xg_full[rows, :] = xg
        sums = lane_sums(xf * xf)
        out[0:256, 0:512] = (dot(xg, wq[...]) + dot(rest, wq[...])).astype(out.dtype)
        out[0:256, 512:640] = (dot(xg, wkv[...], 1, 1) + dot(rest, wkv[...], 1, 1)).astype(out.dtype)
        if k == 0:
            out[256:257, 512:640] = sums[0]
            out[257:258, 512:640] = sums[1]
        else:
            out[256:272, 512:640] = stat_rows(sums, 128)
            out[256:272, 0:512] = jnp.zeros((16, 512), BF16)


def split(v):
    hi = v.astype(BF16)
    return hi, (v - hi.astype(F32)).astype(BF16)


def k_ct(mine, other, w, full, own, m1, m2, m3, cscale):
    y, _, _, _, c = place()
    count = jnp.zeros((16, 512), F32)
    for ref, base in ((mine, c * 512), (other, (1 - c) * 512)):
        for j in range(8):
            full[at(base + j * 64, 64), :] = ref[j * 80 : j * 80 + 64, :]
            count = count + ref[j * 80 + 64 : j * 80 + 80, :].astype(F32)
    cscale[...] = TOKENS / count[0:8, 0:128]
    for k, out in enumerate((own, m1, m2, m3)):
        out[...] = dot(full[at(((y + k) & 3) * 256, 256), :], w[...]).astype(out.dtype)


def k_sum_kv(own, b, c, d, out, kept):
    lanes = slice(512, 640)
    total = sum(r[0:256, lanes].astype(F32) for r in (own, b, c, d))
    stats = [read_stat(r, 256, 2, 512) for r in (b, c, d)]
    sums = [own[256 + i : 257 + i, lanes] + sum(s[i] for s in stats) for i in range(2)]
    write_kv(total, sums, out, kept)


def write_kv(total, sums, out, kept):
    kept[0:256, :] = total
    kept[256:257, :] = sums[0]
    kept[257:258, :] = sums[1]
    out[0:256, :] = total.astype(BF16)
    out[256:272, :] = stat_rows(sums, 128)


def k_sum_heads(p0, p1, p2, p3, d0, d1, d2, d3, *outs):
    zh = place()[1]
    for k, out in enumerate(outs):
        lanes = at(((zh + k) & 3) * 128, 128)
        out[:, 0:128] = sum(r[0:256, lanes].astype(F32) for r in (p0, p1, p2, p3)).astype(out.dtype)
        out[:, 128:256] = sum(r[:, lanes].astype(F32) for r in (d0, d1, d2, d3)).astype(out.dtype)


def k_add_kv(own, got, out, kept):
    stats = read_stat(got, 256, 2)
    sums = [own[256 + i : 257 + i, :] + stats[i] for i in range(2)]
    write_kv(own[0:256, :] + got[0:256, :].astype(F32), sums, out, kept)


def k_kv(own, got, cos, sin, kv, proj, rstd):
    stats = read_stat(got, 256, 2)
    sums = [own[256 + i : 257 + i, :] + stats[i] for i in range(2)]
    scale = columns([lax.rsqrt(s / WIDTH + norm_eps) for s in sums])
    p = own[0:256, :] + got[0:256, :].astype(F32)
    proj[...] = p
    rstd[...] = scale
    v = p * scale
    kv[...] = (v * cos[...] + swap_pairs(v) * sin[...]).astype(BF16)


def k_attend(
    p0, p1, p2, p3, cscale, rstd, cos, sin, kvm, kvo, segments, out, keep, send
):
    scale = DH ** (-0.5)
    y, _, x, zl, c = place()
    sums = sum(r[...].astype(F32) for r in (p0, p1, p2, p3))
    proj = sums[:, 0:128]
    qv = proj * rstd[...]
    q = (qv * cos[...] + swap_pairs(qv) * sin[...]).astype(BF16)
    grad = (sums[:, 128:256] * cscale[0:1, :]).astype(BF16)
    mine, other = kvm[...].astype(F32), kvo[...].astype(F32)
    first = c == 0
    lo, hi = jnp.where(first, mine, other), jnp.where(first, other, mine)
    left = lax.broadcasted_iota(jnp.int32, (TOKENS, 128), 1) < 64
    keys = jnp.where(left, lo, pltpu.roll(hi, 64, 1)).astype(BF16)
    values = jnp.where(left, pltpu.roll(lo, 64, 1), hi).astype(BF16)
    t = token_of(x, zl, lax.broadcasted_iota(jnp.int32, (256, 1), 0) + y * 256)
    start = jnp.zeros((256, 1), jnp.int32)
    for s in (1, 2, 3):
        below = jnp.where(segments[...] < s, 1.0, 0.0)
        begin = jnp.sum(jnp.sum(below, axis=0, keepdims=True), axis=1, keepdims=True)
        begin = begin.astype(jnp.int32)
        start = jnp.where(t >= begin, jnp.maximum(start, begin), start)
    spot = lax.broadcasted_iota(jnp.int32, (1, TOKENS), 1)
    u = token_of(x, zl, ((y - spot // 256) & 3) * 256 + (spot & 255))
    allowed = (u <= t) & (u >= start)
    scores = jnp.where(allowed, dot(q, keys, 1, 1) * scale, -jnp.inf)
    top = jnp.max(scores, axis=1, keepdims=True)
    e = jnp.exp(scores - top)
    probs = e * (1.0 / jnp.sum(e, axis=1, keepdims=True))
    pb = probs.astype(BF16)
    attended = dot(pb, values).astype(BF16)
    out[272:528, :] = attended
    delta = jnp.sum(grad.astype(F32) * attended.astype(F32), axis=1, keepdims=True)
    ds = (probs * (dot(grad, values, 1, 1) - delta)).astype(BF16)
    dq = dot(ds, keys) * scale
    e_q = ((dq * cos[...] - swap_pairs(dq) * sin[...]) * rstd[...]).astype(BF16)
    out[0:256, :] = e_q
    out[256:272, :] = stat_rows(lane_sums(e_q.astype(F32) * proj), 128)
    dk = dot(ds, q, 0, 0) * scale
    dv = dot(pb, grad, 0, 0)
    g_lo = jnp.where(left, dk, pltpu.roll(dv, 64, 1))
    g_hi = jnp.where(left, pltpu.roll(dk, 64, 1), dv)
    keep[...] = jnp.where(first, g_lo, g_hi)
    send[...] = jnp.where(first, g_hi, g_lo).astype(BF16)


def k_dkv_core(keep, got, own, m1, m2, m3):
    for k, out in enumerate((own, m1, m2, m3)):
        rows = slice(k * 256, (k + 1) * 256)
        out[...] = (keep[rows, :] + got[rows, :].astype(F32)).astype(out.dtype)


def k_dkv_sum(own, *refs):
    *got, out, kept = refs
    total = own[...] + sum(r[...].astype(F32) for r in got)
    kept[...] = total
    out[...] = total.astype(BF16)


def k_dkv(own, got, cos, sin, rstd, proj, out):
    g = own[...] + got[...].astype(F32)
    e = ((g * cos[...] - swap_pairs(g) * sin[...]) * rstd[...]).astype(BF16)
    out[0:256, :] = e
    rows = lane_sums(e.astype(F32) * proj[...])
    scales = [rstd[i * 128 : (i + 1) * 128, :].T[0:1, :] for i in range(2)]
    out[256:272, :] = stat_rows(rows + scales, 128)


def k_pack_heads(a, b, cd, out):
    zh = place()[1]
    for head, r, row in ((zh, a, 0), (zh ^ 1, b, 0), (zh ^ 3, cd, 0), (zh ^ 2, cd, 272)):
        out[0:256, at(head * 128, 128)] = r[row : row + 256, :]
    stats = [read_stat(r, 256 + row, 2) for r, row in ((a, 0), (b, 0), (cd, 0), (cd, 272))]
    block = stat_rows([sum(s[i] for s in stats) for i in range(2)], 128)
    for k in range(4):
        out[256:272, k * 128 : (k + 1) * 128] = block


def k_pack_att(a, b, cd, out):
    zh = place()[1]
    for head, r, row in ((zh, a, 272), (zh ^ 1, b, 272), (zh ^ 3, cd, 0), (zh ^ 2, cd, 256)):
        out[:, at(head * 128, 128)] = r[row : row + 256, :]


def k_dnorm(
    q0, q1, q2, q3, k0, k1, k2, k3, wq, wkv, x_full, send, keep, keep_stat, rstd, grad, nsum, rsum
):
    y, _, _, _, c = place()
    gain = jnp.zeros((1, 512), F32)
    for k, (q, kv) in enumerate(((q0, k0), (q1, k1), (q2, k2), (q3, k3))):
        block = (y - k) & 3
        rows = at(block * 256, 256)
        g = dot(q[0:256, :], wq[...], 1, 1) + dot(kv[0:256, :], wkv[...])
        grad[rows, :] = g
        gain = gain + jnp.sum(g * x_full[rows, :].astype(F32), axis=0, keepdims=True)
        nq = read_stat(q, 256, 2)
        nk = read_stat(kv, 256, 4)
        for i in range(2):
            lanes = slice(i * 128, (i + 1) * 128)
            nsum[block, :, lanes] = jnp.broadcast_to(nq[i][:, :128] + nk[i], (8, 128))
            rsum[block, :, lanes] = jnp.broadcast_to(nk[2 + i], (8, 128))
    n = [jnp.concatenate([nsum[2 * h, 0:1, :], nsum[2 * h + 1, 0:1, :]], axis=1) for h in (c, 1 - c)]
    there = at((1 - c) * 512, 512)
    here = at(c * 512, 512)
    send[0:512, :] = grad[there, :].astype(BF16)
    send[512:528, :] = stat_rows([gain, n[1]], 512)
    keep[...] = grad[here, :]
    keep_stat[0:1, :] = gain
    keep_stat[1:2, :] = n[0]
    rstd[...] = rsum[2 * c, :, 0:128]


def k_g_core(keep, keep_stat, got, m0, m1, m2, m3):
    gain, n = read_stat(got, 512, 2)
    gain = gain + keep_stat[0:1, :]
    n = n + keep_stat[1:2, :]
    for k, out in enumerate((m0, m1, m2, m3)):
        rows = slice(k * 128, (k + 1) * 128)
        out[0:128, :] = (keep[rows, :] + got[rows, :].astype(F32)).astype(BF16)
        part = jnp.concatenate([n[:, k * 128 : (k + 1) * 128], jnp.zeros((1, 384), F32)], axis=1)
        out[128:144, :] = stat_rows([gain, part], 512)


def k_g_x(a, b, c, d, keep, send):
    refs = (a, b, c, d)
    stats = [read_stat(r, 128, 2) for r in refs]
    gain, n = (sum(s[i] for s in stats) for i in range(2))
    total = sum(r[0:128, :].astype(F32) for r in refs)
    keep[0:64, :] = total[0:64]
    keep[64:65, :] = gain
    keep[65:66, :] = n
    send[0:64, :] = total[64:128].astype(BF16)
    n_there = jnp.concatenate([n[:, 64:128], n[:, 0:64], n[:, 128:512]], axis=1)
    send[64:80, :] = stat_rows([gain, n_there], 512)


def k_final(keep, got, x, ct, gain_in, cscale, rstd, res, gain, inner):
    stats = read_stat(got, 64, 2)
    gain[...] = keep[64:65, :] + stats[0]
    n = (keep[65:66, :] + stats[1])[:, 0:128]
    inner[...] = n[:, 0:64]
    scale = rstd[0:1, :]
    corr = columns([scale * scale * n * (1.0 / WIDTH)])[0:64]
    g = keep[0:64, :] + got[0:64, :].astype(F32)
    for j in range(4):
        lanes = slice(j * 128, (j + 1) * 128)
        scaled = (ct[0:64, lanes].astype(F32) * cscale[0:1, :]).astype(BF16).astype(F32)
        res[:, lanes] = (
            scaled + g[:, lanes] * gain_in[:, lanes] - x[:, lanes].astype(F32) * corr
        ).astype(BF16)


def k_grad_w(xg_full, q0, q1, q2, q3, k0, k1, k2, k3, gq, gk, gv):
    y = place()[0]
    gkv = jnp.zeros((128, 512), F32)
    for k, (q, kv) in enumerate(((q0, k0), (q1, k1), (q2, k2), (q3, k3))):
        left = xg_full[at(((y - k) & 3) * 256, 256), :]
        part = dot(left, q[0:256, :], 0, 0)
        gq[...] = part if k == 0 else gq[...] + part
        gkv = gkv + dot(kv[0:256, :], left, 0, 0)
    gk[...] = gkv[0:64]
    gv[...] = gkv[64:128]


def k_grad_o(ct_full, a, b, c, d, cscale, go):
    y = place()[0]
    for k, r in enumerate((a, b, c, d)):
        part = dot(ct_full[at(((y - k) & 3) * 256, 256), :], r[...], 0, 0)
        go[...] = part if k == 0 else go[...] + part
    go[...] = go[...] * cscale[0:1, 0:1]


def shards(hidden, gain, wq, wk, wv, wo, cotangent, mask, segments):
    gain2 = gain[None, :]
    order = Order()
    table = ((256, 128), F32)

    x_got = shift(hidden, "zl")
    ct0, wkv, cos_q, sin_q, cos_k, sin_k = call(
        k_prep,
        [((80, 512), BF16), ((128, 512), BF16)] + [table] * 4,
        cotangent, mask[None, :], wk.T, wv.T,
    )
    ct_got = shift(ct0, "zl")
    xs = jnp.concatenate([hidden, order.after(x_got, ct0)], axis=0)
    x_parts = spread([xs] * 4, "x")
    x_parts[0] = order.after(x_parts[0], ct_got)
    x_mine = jnp.concatenate([xs, *x_parts], axis=0)
    x_other = shift(x_mine, "c")
    cs = jnp.concatenate([ct0, order.after(ct_got, *x_parts)], axis=0)
    ct_parts = spread([cs] * 4, "x")

    message = ((272, 128), BF16)
    own_kv = ((264, 128), F32)
    x_full, xg_full, p_own, *p_part = call(
        k_proj,
        [((1024, 512), BF16)] * 2 + [((264, 640), F32)] + [((272, 640), BF16)] * 3,
        x_mine, x_other, gain2, wq, wkv,
    )
    p_got = spread([None, *p_part], "y")
    ct_mine = jnp.concatenate([cs, *[order.after(part, *p_got) for part in ct_parts]], axis=0)
    ct_other = shift(ct_mine, "c")
    ct_full, d_own, d1, d2, d3, cscale = call(
        k_ct,
        [((1024, 512), BF16), ((256, 512), F32)] + [((256, 512), BF16)] * 3 + [((8, 128), F32)],
        ct_mine, ct_other, wo,
    )
    kv_sum, kv_kept = call(k_sum_kv, [message, own_kv], p_own, *p_got)
    kv_next = pair(kv_sum, "zh", 1)
    d_got = spread([None] + [order.after(part, kv_next) for part in (d1, d2, d3)], "y")
    kv_sum, kv_kept = call(
        k_add_kv, [message, own_kv], order.after(kv_kept, d1), kv_next
    )
    kv_next = pair(kv_sum, "zh", 3)
    heads = call(
        k_sum_heads,
        [((256, 256), F32)] + [((256, 256), BF16)] * 3,
        p_own, *p_got, d_own, *d_got,
    )
    heads = [heads[0], *spread(heads, "zh")]
    kv, proj_kv, rstd = call(
        k_kv, [((256, 128), BF16), table, table], kv_kept, kv_next, cos_k, sin_k
    )
    kv_parts = spread([kv] * 4, "y")
    kv_parts[0] = order.after(kv_parts[0], *heads[1:])
    kv_mine = jnp.concatenate([kv, *kv_parts], axis=0)
    kv_other = shift(kv_mine, "c")

    eq, keep, send = call(
        k_attend,
        [((528, 128), BF16), ((1024, 128), F32), ((1024, 128), BF16)],
        *heads, cscale, rstd, cos_q, sin_q, kv_mine, kv_other, segments.reshape(8, 128),
        unread=order.take(),
    )
    dkv_own, *dkv = call(k_dkv_core, [table] + [((256, 128), BF16)] * 3, keep, shift(send, "c"))
    dkv_got = spread([None, *dkv], "y", -1)
    eq_next = order.after(pair(eq, "zh", 1), *dkv_got)
    eq_two = pair(jnp.concatenate([eq[:272], eq_next[:272]], axis=0), "zh", 3)
    small = [((256, 128), BF16), table]
    dkv_sum, dkv_kept = call(k_dkv_sum, small, dkv_own, *dkv_got)
    dkv_next = pair(dkv_sum, "zh", 1)
    (eq_row,) = call(k_pack_heads, [((272, 512), BF16)], eq, eq_next, eq_two)
    eq_rows = [eq_row, *spread([eq_row] * 4, "y")]
    dkv_sum, dkv_kept = call(k_dkv_sum, small, dkv_kept, dkv_next)
    dkv_next = pair(dkv_sum, "zh", 3)
    att_cat = jnp.concatenate([eq[272:], eq_next[272:]], axis=0)
    att_two = pair(order.after(att_cat, dkv_sum), "zh", 3)
    (ekv,) = call(k_dkv, [message], dkv_kept, dkv_next, cos_k, sin_k, rstd, proj_kv)
    ekv_rows = [ekv, *spread([ekv] * 4, "y")]

    ekv_rows[1] = order.after(ekv_rows[1], att_two)
    send_g, keep_g, keep_stat, rstd_col = call(
        k_dnorm,
        [((528, 512), BF16), ((512, 512), F32), ((8, 512), F32), ((8, 128), F32)],
        *eq_rows, *ekv_rows, wq, wkv, x_full,
        scratch=[
            pltpu.VMEM((1024, 512), F32),
            pltpu.VMEM((4, 8, 256), F32),
            pltpu.VMEM((4, 8, 256), F32),
        ],
        unread=order.take(),
    )
    (att_row,) = call(k_pack_att, [((256, 512), BF16)], eq, eq_next, order.after(att_two, send_g))
    att_rows = [att_row, *spread([att_row] * 4, "y")]
    got_g = shift(send_g, "c")
    g_parts = call(k_g_core, [((144, 512), BF16)] * 4, keep_g, keep_stat, got_g)
    g_got = spread(g_parts, "x", -1)
    gq, gk, gv = call(
        k_grad_w,
        [((512, 512), F32), ((64, 512), F32), ((64, 512), F32)],
        xg_full, *eq_rows, *ekv_rows,
    )
    keep_z, send_z = call(k_g_x, [((72, 512), F32), ((80, 512), BF16)], g_parts[0], *g_got)
    got_z = shift(send_z, "zl")
    (go,) = call(k_grad_o, [((512, 512), F32)], ct_full, *att_rows, cscale)
    res, gain_grad, inner = call(
        k_final,
        [((64, 512), BF16), ((1, 512), F32), ((1, 64), F32)],
        keep_z, got_z, hidden, ct0, gain2, cscale, rstd_col,
        unread=order.take(),
    )
    return res, gain_grad[0], gq, gk.T, gv.T, go, inner[0]


def solution(mesh):
    return jax.shard_map(
        shards,
        mesh=mesh,
        in_specs=(
            P("col", "row"),
            P("row"),
            P("row", "col"),
            P("row", "col"),
            P("row", "col"),
            P("row", "col"),
            P("col", "row"),
            P("col"),
            P(),
        ),
        out_specs=(
            P("col", "row"),
            P("row"),
            P("row", "col"),
            P("row", "col"),
            P("row", "col"),
            P("row", "col"),
            P("col"),
        ),
        check_vma=False,
    )
```

```python
import math

import jax
import jax.numpy as jnp
from jax import lax
from jax.experimental import pallas as pl
from jax.experimental.pallas import tpu as pltpu
from jax.sharding import PartitionSpec as P

DH = 128
WIDTH = 8192
TOKENS = 1024
rope_theta = 500000.0
norm_eps = 1e-05
F32 = jnp.float32
BF16 = jnp.bfloat16

STEPS = {
    "y": ("row", lambda i, k: (i // 4 + k) % 4 * 4 + i % 4),
    "zh": ("row", lambda i, k: i // 4 * 4 + (i % 4 + k) % 4),
    "x": ("col", lambda i, k: (i // 4 + k) % 4 * 4 + i % 4),
    "zl": ("col", lambda i, k: i ^ 2),
    "c": ("col", lambda i, k: i ^ 1),
}


def shift(array, axis, k=1):
    name, place = STEPS[axis]
    return lax.ppermute(array, name, [(i, place(i, k)) for i in range(16)])


def spread(arrays, axis, sign=1):
    got = {k: shift(arrays[k], axis, (sign * k) % 4) for k in (1, 3, 2)}
    return [got[1], got[2], got[3]]


def pair(array, axis, k):
    name, _ = STEPS[axis]
    low = 1 if axis == "zh" else 4
    return lax.ppermute(array, name, [(i, i ^ (k * low)) for i in range(16)])


def call(body, outs, *args, scratch=(), unread=()):
    def whole(*refs):
        body(*refs[: len(args)], *refs[len(args) + len(unread) :])

    return pl.pallas_call(
        whole,
        out_shape=[jax.ShapeDtypeStruct(s, d) for s, d in outs],
        in_specs=[pl.BlockSpec(memory_space=pltpu.VMEM)] * len(args)
        + [pl.BlockSpec(memory_space=pl.ANY)] * len(unread),
        out_specs=[pl.BlockSpec(memory_space=pltpu.VMEM)] * len(outs),
        scratch_shapes=list(scratch),
        compiler_params=pltpu.CompilerParams(vmem_limit_bytes=40 * 1024 * 1024),
        name=body.__name__,
    )(*args, *unread)


class Order:
    def __init__(self):
        self.kept = []

    def after(self, value, *others):
        value, *others = lax.optimization_barrier((value, *others))
        self.kept += others
        return value

    def take(self):
        kept, self.kept = self.kept, []
        return kept


def place():
    row, col = lax.axis_index("row"), lax.axis_index("col")
    return row // 4, row % 4, col // 4, col // 2 % 2, col % 2


def dot(a, b, ca=1, cb=0):
    return lax.dot_general(a, b, (((ca,), (cb,)), ((), ())), preferred_element_type=F32)


def at(base, size):
    return pl.ds(pl.multiple_of(base, size), size)


def halves(row):
    hi = row.astype(BF16).astype(F32)
    return hi, row - hi


def stat_rows(rows, lanes):
    place = lax.broadcasted_iota(jnp.int32, (16, lanes), 0)
    out = jnp.zeros((16, lanes), F32)
    for i, row in enumerate(rows):
        hi, lo = halves(row)
        out = jnp.where(place == 2 * i, hi, out)
        out = jnp.where(place == 2 * i + 1, lo, out)
    return out.astype(BF16)


def read_stat(ref, start, count, lane=0):
    block = ref[start : start + 16, lane:].astype(F32)
    return [block[2 * i : 2 * i + 1] + block[2 * i + 1 : 2 * i + 2] for i in range(count)]


def lane_sums(values):
    part = values[:, :128]
    for j in range(1, values.shape[1] // 128):
        part = part + values[:, j * 128 : (j + 1) * 128]
    return [
        jnp.sum(part[i * 128 : (i + 1) * 128].T, axis=0, keepdims=True)
        for i in range(values.shape[0] // 128)
    ]


def columns(rows):
    return jnp.concatenate([jnp.broadcast_to(r, (128, 128)).T for r in rows], axis=0)


def swap_pairs(v):
    even = lax.broadcasted_iota(jnp.int32, v.shape, 1) % 2 == 0
    return jnp.where(even, pltpu.roll(v, 127, 1), pltpu.roll(v, 1, 1))


def token_of(x, zl, spot):
    there = (x - (spot // 128) % 4) & 3
    return there * 256 + (zl ^ ((spot // 64) & 1)) * 128 + (spot // 512) * 64 + (spot & 63)


def k_prep(cotangent, mask, segments, ct, begin, cos, sin, cos_k, sin_k):
    y, _, x, zl, c = place()
    m = mask[...].astype(F32)
    column = jnp.broadcast_to(jnp.concatenate([m, m], axis=1), (128, 128)).T[0:64]
    for j in range(4):
        lanes = slice(j * 128, (j + 1) * 128)
        ct[0:64, lanes] = jnp.where(column > 0, cotangent[:, lanes].astype(F32), 0.0).astype(BF16)
    count = jnp.sum(m, axis=1, keepdims=True)
    ct[64:80, :] = jnp.broadcast_to(count, (16, 512)).astype(BF16)
    for s in (1, 2, 3):
        below = jnp.where(segments[...] < s, 1.0, 0.0)
        total = jnp.sum(jnp.sum(below, axis=0, keepdims=True), axis=1, keepdims=True)
        begin[s : s + 1, :] = jnp.broadcast_to(total, (1, 128))
    lane = lax.broadcasted_iota(jnp.int32, (1, 128), 1)
    rate = jnp.exp((lane // 2).astype(F32) * (-2.0 * math.log(rope_theta) / DH))
    spot = lax.broadcasted_iota(jnp.int32, (256, 1), 0) + y * 256
    angle = token_of(x, zl, spot).astype(F32) * rate
    co, si = jnp.cos(angle), jnp.sin(angle)
    si = jnp.where(lane % 2 == 0, -si, si)
    cos[...] = co
    sin[...] = si
    cos_k[...] = jnp.where(lane < 64, jnp.where(c == 0, co, pltpu.roll(co, 64, 1)), 1.0)
    sin_k[...] = jnp.where(lane < 64, jnp.where(c == 0, si, pltpu.roll(si, 64, 1)), 0.0)


def k_proj(mine, other, gain, wq, wk, wv, wkv, x_full, xg_full, *outs):
    y, _, _, _, c = place()
    wkv[0:64, :] = wk[...]
    wkv[64:128, :] = wv[...]
    x_full[at(c * 512, 512), :] = mine[...]
    x_full[at((1 - c) * 512, 512), :] = other[...]
    for k, (kv, q) in enumerate(zip(outs[:4], outs[4:])):
        rows = at(((y + k) & 3) * 256, 256)
        xf = x_full[rows, :].astype(F32)
        xg, rest = split(xf * gain[...])
        xg_full[rows, :] = xg
        sums = lane_sums(xf * xf)
        q[...] = (dot(xg, wq[...]) + dot(rest, wq[...])).astype(q.dtype)
        kv[0:256, :] = (dot(xg, wkv[...], 1, 1) + dot(rest, wkv[...], 1, 1)).astype(kv.dtype)
        if k == 0:
            kv[256:257, :] = sums[0]
            kv[257:258, :] = sums[1]
        else:
            kv[256:272, :] = stat_rows(sums, 128)


def split(v):
    hi = v.astype(BF16)
    return hi, (v - hi.astype(F32)).astype(BF16)


def k_ct(mine, other, w, full, own, m1, m2, m3, cscale):
    y, _, _, _, c = place()
    count = jnp.zeros((16, 512), F32)
    for ref, base in ((mine, c * 512), (other, (1 - c) * 512)):
        for j in range(8):
            full[at(base + j * 64, 64), :] = ref[j * 80 : j * 80 + 64, :]
            count = count + ref[j * 80 + 64 : j * 80 + 80, :].astype(F32)
    cscale[...] = TOKENS / count[0:8, 0:128]
    for k, out in enumerate((own, m1, m2, m3)):
        out[...] = dot(full[at(((y + k) & 3) * 256, 256), :], w[...]).astype(out.dtype)


def k_sum_kv(own, *refs):
    *got, out, kept = refs
    total = own[0:256, :] + sum(r[0:256, :].astype(F32) for r in got)
    stats = [read_stat(r, 256, 2) for r in got]
    sums = [own[256 + i : 257 + i, :] + sum(s[i] for s in stats) for i in range(2)]
    write_kv(total, sums, out, kept)


def write_kv(total, sums, out, kept):
    kept[0:256, :] = total
    kept[256:257, :] = sums[0]
    kept[257:258, :] = sums[1]
    out[0:256, :] = total.astype(BF16)
    out[256:272, :] = stat_rows(sums, 128)


def k_sum_heads(p0, p1, p2, p3, d0, d1, d2, d3, *outs):
    zh = place()[1]
    for k, out in enumerate(outs):
        lanes = at(((zh + k) & 3) * 128, 128)
        out[:, 0:128] = sum(r[:, lanes].astype(F32) for r in (p0, p1, p2, p3)).astype(out.dtype)
        out[:, 128:256] = sum(r[:, lanes].astype(F32) for r in (d0, d1, d2, d3)).astype(out.dtype)


def k_kv(own, got, cos, sin, kv, proj, rstd):
    stats = read_stat(got, 256, 2)
    sums = [own[256 + i : 257 + i, :] + stats[i] for i in range(2)]
    scale = columns([lax.rsqrt(s / WIDTH + norm_eps) for s in sums])
    p = own[0:256, :] + got[0:256, :].astype(F32)
    proj[...] = p
    rstd[...] = scale
    v = p * scale
    kv[...] = (v * cos[...] + swap_pairs(v) * sin[...]).astype(BF16)


def k_attend(
    p0, p1, p2, p3, cscale, rstd, cos, sin, kvm, kvo, begins, out, keep, send
):
    scale = DH ** (-0.5)
    y, _, x, zl, c = place()
    sums = sum(r[...].astype(F32) for r in (p0, p1, p2, p3))
    proj = sums[:, 0:128]
    qv = proj * rstd[...]
    q = (qv * cos[...] + swap_pairs(qv) * sin[...]).astype(BF16)
    grad = (sums[:, 128:256] * cscale[0:1, :]).astype(BF16)
    mine, other = kvm[...].astype(F32), kvo[...].astype(F32)
    first = c == 0
    lo, hi = jnp.where(first, mine, other), jnp.where(first, other, mine)
    left = lax.broadcasted_iota(jnp.int32, (TOKENS, 128), 1) < 64
    keys = jnp.where(left, lo, pltpu.roll(hi, 64, 1)).astype(BF16)
    values = jnp.where(left, pltpu.roll(lo, 64, 1), hi).astype(BF16)
    t = token_of(x, zl, lax.broadcasted_iota(jnp.int32, (256, 1), 0) + y * 256)
    start = jnp.zeros((256, 1), jnp.int32)
    for s in (1, 2, 3):
        begin = begins[s : s + 1, 0:1].astype(jnp.int32)
        start = jnp.where(t >= begin, jnp.maximum(start, begin), start)
    spot = lax.broadcasted_iota(jnp.int32, (1, TOKENS), 1)
    u = token_of(x, zl, ((y - spot // 256) & 3) * 256 + (spot & 255))
    allowed = (u <= t) & (u >= start)
    scores = jnp.where(allowed, dot(q, keys, 1, 1) * scale, -jnp.inf)
    top = jnp.max(scores, axis=1, keepdims=True)
    e = jnp.exp(scores - top)
    probs = e * (1.0 / jnp.sum(e, axis=1, keepdims=True))
    pb = probs.astype(BF16)
    attended = dot(pb, values).astype(BF16)
    out[272:528, :] = attended
    delta = jnp.sum(grad.astype(F32) * attended.astype(F32), axis=1, keepdims=True)
    ds = (probs * (dot(grad, values, 1, 1) - delta)).astype(BF16)
    dq = dot(ds, keys) * scale
    e_q = ((dq * cos[...] - swap_pairs(dq) * sin[...]) * rstd[...]).astype(BF16)
    out[0:256, :] = e_q
    out[256:272, :] = stat_rows(lane_sums(e_q.astype(F32) * proj), 128)
    dk = dot(ds, q, 0, 0) * scale
    dv = dot(pb, grad, 0, 0)
    g_lo = jnp.where(left, dk, pltpu.roll(dv, 64, 1))
    g_hi = jnp.where(left, pltpu.roll(dk, 64, 1), dv)
    keep[...] = jnp.where(first, g_lo, g_hi)
    send[...] = jnp.where(first, g_hi, g_lo).astype(BF16)


def k_dkv_core(keep, got, own, m1, m2, m3):
    for k, out in enumerate((own, m1, m2, m3)):
        rows = slice(k * 256, (k + 1) * 256)
        out[...] = (keep[rows, :] + got[rows, :].astype(F32)).astype(out.dtype)


def k_dkv_sum(own, *refs):
    *got, out, kept = refs
    total = own[...] + sum(r[...].astype(F32) for r in got)
    kept[...] = total
    out[...] = total.astype(BF16)


def k_dkv(own, got, cos, sin, rstd, proj, out):
    g = own[...] + got[...].astype(F32)
    e = ((g * cos[...] - swap_pairs(g) * sin[...]) * rstd[...]).astype(BF16)
    out[0:256, :] = e
    rows = lane_sums(e.astype(F32) * proj[...])
    scales = [rstd[i * 128 : (i + 1) * 128, :].T[0:1, :] for i in range(2)]
    out[256:272, :] = stat_rows(rows + scales, 128)


def k_pack_heads(a, b, cd, out):
    zh = place()[1]
    for head, r, row in ((zh, a, 0), (zh ^ 1, b, 0), (zh ^ 3, cd, 0), (zh ^ 2, cd, 272)):
        out[0:256, at(head * 128, 128)] = r[row : row + 256, :]
    stats = [read_stat(r, 256 + row, 2) for r, row in ((a, 0), (b, 0), (cd, 0), (cd, 272))]
    block = stat_rows([sum(s[i] for s in stats) for i in range(2)], 128)
    for k in range(4):
        out[256:272, k * 128 : (k + 1) * 128] = block


def k_pack_att(a, b, cd, out):
    zh = place()[1]
    for head, r, row in ((zh, a, 272), (zh ^ 1, b, 272), (zh ^ 3, cd, 0), (zh ^ 2, cd, 256)):
        out[:, at(head * 128, 128)] = r[row : row + 256, :]


def k_dnorm(
    q0, q1, q2, q3, k0, k1, k2, k3, wq, wkv, x_full, send, keep, keep_stat, rstd, grad, nsum, rsum
):
    y, _, _, _, c = place()
    gain = jnp.zeros((1, 512), F32)
    for k, (q, kv) in enumerate(((q0, k0), (q1, k1), (q2, k2), (q3, k3))):
        block = (y - k) & 3
        rows = at(block * 256, 256)
        g = dot(q[0:256, :], wq[...], 1, 1) + dot(kv[0:256, :], wkv[...])
        grad[rows, :] = g
        gain = gain + jnp.sum(g * x_full[rows, :].astype(F32), axis=0, keepdims=True)
        nq = read_stat(q, 256, 2)
        nk = read_stat(kv, 256, 4)
        for i in range(2):
            lanes = slice(i * 128, (i + 1) * 128)
            nsum[block, :, lanes] = jnp.broadcast_to(nq[i][:, :128] + nk[i], (8, 128))
            rsum[block, :, lanes] = jnp.broadcast_to(nk[2 + i], (8, 128))
    n = [jnp.concatenate([nsum[2 * h, 0:1, :], nsum[2 * h + 1, 0:1, :]], axis=1) for h in (c, 1 - c)]
    there = at((1 - c) * 512, 512)
    here = at(c * 512, 512)
    send[0:512, :] = grad[there, :].astype(BF16)
    send[512:528, :] = stat_rows([gain, n[1]], 512)
    keep[...] = grad[here, :]
    keep_stat[0:1, :] = gain
    keep_stat[1:2, :] = n[0]
    rstd[...] = rsum[2 * c, :, 0:128]


def k_g_core(keep, keep_stat, got, m0, m1, m2, m3):
    gain, n = read_stat(got, 512, 2)
    gain = gain + keep_stat[0:1, :]
    n = n + keep_stat[1:2, :]
    for k, out in enumerate((m0, m1, m2, m3)):
        rows = slice(k * 128, (k + 1) * 128)
        out[0:128, :] = (keep[rows, :] + got[rows, :].astype(F32)).astype(BF16)
        part = jnp.concatenate([n[:, k * 128 : (k + 1) * 128], jnp.zeros((1, 384), F32)], axis=1)
        out[128:144, :] = stat_rows([gain, part], 512)


def k_g_x(a, b, c, d, keep, send):
    refs = (a, b, c, d)
    stats = [read_stat(r, 128, 2) for r in refs]
    gain, n = (sum(s[i] for s in stats) for i in range(2))
    total = sum(r[0:128, :].astype(F32) for r in refs)
    keep[0:64, :] = total[0:64]
    keep[64:65, :] = gain
    keep[65:66, :] = n
    send[0:64, :] = total[64:128].astype(BF16)
    n_there = jnp.concatenate([n[:, 64:128], n[:, 0:64], n[:, 128:512]], axis=1)
    send[64:80, :] = stat_rows([gain, n_there], 512)


def k_final(keep, got, x, ct, gain_in, cscale, rstd, res, gain, inner):
    stats = read_stat(got, 64, 2)
    gain[...] = keep[64:65, :] + stats[0]
    n = (keep[65:66, :] + stats[1])[:, 0:128]
    inner[...] = n[:, 0:64]
    scale = rstd[0:1, :]
    corr = columns([scale * scale * n * (1.0 / WIDTH)])[0:64]
    g = keep[0:64, :] + got[0:64, :].astype(F32)
    for j in range(4):
        lanes = slice(j * 128, (j + 1) * 128)
        scaled = (ct[0:64, lanes].astype(F32) * cscale[0:1, :]).astype(BF16).astype(F32)
        res[:, lanes] = (
            scaled + g[:, lanes] * gain_in[:, lanes] - x[:, lanes].astype(F32) * corr
        ).astype(BF16)


def k_grad_w(xg_full, q0, q1, q2, q3, k0, k1, k2, k3, gq, gk, gv):
    y = place()[0]
    gkv = jnp.zeros((128, 512), F32)
    for k, (q, kv) in enumerate(((q0, k0), (q1, k1), (q2, k2), (q3, k3))):
        left = xg_full[at(((y - k) & 3) * 256, 256), :]
        part = dot(left, q[0:256, :], 0, 0)
        gq[...] = part if k == 0 else gq[...] + part
        gkv = gkv + dot(kv[0:256, :], left, 0, 0)
    gk[...] = gkv[0:64]
    gv[...] = gkv[64:128]


def k_grad_o(ct_full, a, b, c, d, cscale, go):
    y = place()[0]
    for k, r in enumerate((a, b, c, d)):
        part = dot(ct_full[at(((y - k) & 3) * 256, 256), :], r[...], 0, 0)
        go[...] = part if k == 0 else go[...] + part
    go[...] = go[...] * cscale[0:1, 0:1]


def shards(hidden, gain, wq, wk, wv, wo, cotangent, mask, segments):
    gain2 = gain[None, :]
    order = Order()
    table = ((256, 128), F32)

    x_got = shift(hidden, "zl")
    ct0, begin, cos_q, sin_q, cos_k, sin_k = call(
        k_prep,
        [((80, 512), BF16), ((8, 128), F32)] + [table] * 4,
        cotangent, mask[None, :], segments.reshape(8, 128),
    )
    ct_got = shift(ct0, "zl")
    xs = jnp.concatenate([hidden, order.after(x_got, ct0)], axis=0)
    x_parts = spread([xs] * 4, "x")
    x_parts[0] = order.after(x_parts[0], ct_got)
    x_mine = jnp.concatenate([xs, *x_parts], axis=0)
    x_other = shift(x_mine, "c")
    cs = jnp.concatenate([ct0, order.after(ct_got, *x_parts)], axis=0)
    ct_parts = spread([cs] * 4, "x")

    message = ((272, 128), BF16)
    own_kv = ((264, 128), F32)
    wkv, x_full, xg_full, kv_own, *parts = call(
        k_proj,
        [((128, 512), BF16)]
        + [((1024, 512), BF16)] * 2
        + [own_kv] + [message] * 3
        + [((256, 512), F32)] + [((256, 512), BF16)] * 3,
        x_mine, x_other, gain2, wq, wk.T, wv.T,
    )
    kv_got = spread([None, *parts[:3]], "y")
    p_own, *p_part = parts[3:]
    p_got = spread([None, *[order.after(part, *kv_got) for part in p_part]], "y")
    ct_mine = jnp.concatenate([cs, *[order.after(part, *kv_got) for part in ct_parts]], axis=0)
    ct_other = shift(ct_mine, "c")
    ct_full, d_own, d1, d2, d3, cscale = call(
        k_ct,
        [((1024, 512), BF16), ((256, 512), F32)] + [((256, 512), BF16)] * 3 + [((8, 128), F32)],
        ct_mine, ct_other, wo,
    )
    kv_sum, kv_kept = call(k_sum_kv, [message, own_kv], kv_own, *kv_got)
    kv_next = pair(kv_sum, "zh", 1)
    d_got = spread([None] + [order.after(part, kv_next) for part in (d1, d2, d3)], "y")
    kv_sum, kv_kept = call(
        k_sum_kv, [message, own_kv], order.after(kv_kept, d1), kv_next
    )
    kv_next = pair(kv_sum, "zh", 3)
    heads = call(
        k_sum_heads,
        [((256, 256), F32)] + [((256, 256), BF16)] * 3,
        p_own, *p_got, d_own, *d_got,
    )
    heads = [heads[0], *spread(heads, "zh")]
    kv, proj_kv, rstd = call(
        k_kv, [((256, 128), BF16), table, table], kv_kept, kv_next, cos_k, sin_k
    )
    kv_parts = spread([kv] * 4, "y")
    kv_parts[0] = order.after(kv_parts[0], *heads[1:])
    kv_mine = jnp.concatenate([kv, *kv_parts], axis=0)
    kv_other = shift(kv_mine, "c")

    eq, keep, send = call(
        k_attend,
        [((528, 128), BF16), ((1024, 128), F32), ((1024, 128), BF16)],
        *heads, cscale, rstd, cos_q, sin_q, kv_mine, kv_other, begin,
        unread=order.take(),
    )
    dkv_own, *dkv = call(k_dkv_core, [table] + [((256, 128), BF16)] * 3, keep, shift(send, "c"))
    dkv_got = spread([None, *dkv], "y", -1)
    eq_next = order.after(pair(eq, "zh", 1), *dkv_got)
    eq_two = pair(jnp.concatenate([eq[:272], eq_next[:272]], axis=0), "zh", 3)
    small = [((256, 128), BF16), table]
    dkv_sum, dkv_kept = call(k_dkv_sum, small, dkv_own, *dkv_got)
    dkv_next = pair(dkv_sum, "zh", 1)
    (eq_row,) = call(k_pack_heads, [((272, 512), BF16)], eq, eq_next, eq_two)
    eq_rows = [eq_row, *spread([eq_row] * 4, "y")]
    dkv_sum, dkv_kept = call(k_dkv_sum, small, dkv_kept, dkv_next)
    dkv_next = pair(dkv_sum, "zh", 3)
    att_cat = jnp.concatenate([eq[272:], eq_next[272:]], axis=0)
    att_two = pair(order.after(att_cat, dkv_sum), "zh", 3)
    (ekv,) = call(k_dkv, [message], dkv_kept, dkv_next, cos_k, sin_k, rstd, proj_kv)
    ekv_rows = [ekv, *spread([ekv] * 4, "y")]

    ekv_rows[1] = order.after(ekv_rows[1], att_two)
    send_g, keep_g, keep_stat, rstd_col = call(
        k_dnorm,
        [((528, 512), BF16), ((512, 512), F32), ((8, 512), F32), ((8, 128), F32)],
        *eq_rows, *ekv_rows, wq, wkv, x_full,
        scratch=[
            pltpu.VMEM((1024, 512), F32),
            pltpu.VMEM((4, 8, 256), F32),
            pltpu.VMEM((4, 8, 256), F32),
        ],
        unread=order.take(),
    )
    (att_row,) = call(k_pack_att, [((256, 512), BF16)], eq, eq_next, order.after(att_two, *ekv_rows))
    att_rows = [att_row, *spread([att_row] * 4, "y")]
    got_g = shift(send_g, "c")
    g_parts = call(k_g_core, [((144, 512), BF16)] * 4, keep_g, keep_stat, got_g)
    g_got = spread(g_parts, "x", -1)
    gq, gk, gv = call(
        k_grad_w,
        [((512, 512), F32), ((64, 512), F32), ((64, 512), F32)],
        xg_full, *eq_rows, *ekv_rows,
    )
    keep_z, send_z = call(k_g_x, [((72, 512), F32), ((80, 512), BF16)], g_parts[0], *g_got)
    got_z = shift(send_z, "zl")
    (go,) = call(k_grad_o, [((512, 512), F32)], ct_full, *att_rows, cscale)
    res, gain_grad, inner = call(
        k_final,
        [((64, 512), BF16), ((1, 512), F32), ((1, 64), F32)],
        keep_z, got_z, hidden, ct0, gain2, cscale, rstd_col,
        unread=order.take(),
    )
    return res, gain_grad[0], gq, gk.T, gv.T, go, inner[0]


def solution(mesh):
    return jax.shard_map(
        shards,
        mesh=mesh,
        in_specs=(
            P("col", "row"),
            P("row"),
            P("row", "col"),
            P("row", "col"),
            P("row", "col"),
            P("row", "col"),
            P("col", "row"),
            P("col"),
            P(),
        ),
        out_specs=(
            P("col", "row"),
            P("row"),
            P("row", "col"),
            P("row", "col"),
            P("row", "col"),
            P("row", "col"),
            P("col"),
        ),
        check_vma=False,
    )
```

```python
import math

import jax
import jax.numpy as jnp
from jax import lax
from jax.experimental import pallas as pl
from jax.experimental.pallas import tpu as pltpu
from jax.sharding import PartitionSpec as P

DH = 128
WIDTH = 8192
TOKENS = 1024
rope_theta = 500000.0
norm_eps = 1e-05
F32 = jnp.float32
BF16 = jnp.bfloat16

STEPS = {
    "y": ("row", lambda i, k: (i // 4 + k) % 4 * 4 + i % 4),
    "zh": ("row", lambda i, k: i // 4 * 4 + (i % 4 + k) % 4),
    "x": ("col", lambda i, k: (i // 4 + k) % 4 * 4 + i % 4),
    "zl": ("col", lambda i, k: i ^ 2),
    "c": ("col", lambda i, k: i ^ 1),
}


def shift(array, axis, k=1):
    name, place = STEPS[axis]
    return lax.ppermute(array, name, [(i, place(i, k)) for i in range(16)])


def spread(arrays, axis, sign=1, give=(1, 2, 3)):
    got = {k: shift(arrays[k], axis, (sign * k) % 4) for k in (1, 3, 2)}
    return [got[k] for k in give]


def pair(array, axis, k):
    name, _ = STEPS[axis]
    low = 1 if axis == "zh" else 4
    return lax.ppermute(array, name, [(i, i ^ (k * low)) for i in range(16)])


def call(body, outs, *args, scratch=(), unread=()):
    def whole(*refs):
        body(*refs[: len(args)], *refs[len(args) + len(unread) :])

    return pl.pallas_call(
        whole,
        out_shape=[jax.ShapeDtypeStruct(s, d) for s, d in outs],
        in_specs=[pl.BlockSpec(memory_space=pltpu.VMEM)] * len(args)
        + [pl.BlockSpec(memory_space=pl.ANY)] * len(unread),
        out_specs=[pl.BlockSpec(memory_space=pltpu.VMEM)] * len(outs),
        scratch_shapes=list(scratch),
        compiler_params=pltpu.CompilerParams(vmem_limit_bytes=40 * 1024 * 1024),
        name=body.__name__,
    )(*args, *unread)


class Order:
    def __init__(self):
        self.kept = []

    def after(self, value, *others):
        value, *others = lax.optimization_barrier((value, *others))
        self.kept += others
        return value

    def take(self):
        kept, self.kept = self.kept, []
        return kept


def place():
    row, col = lax.axis_index("row"), lax.axis_index("col")
    return row // 4, row % 4, col // 4, col // 2 % 2, col % 2


def dot(a, b, ca=1, cb=0):
    return lax.dot_general(a, b, (((ca,), (cb,)), ((), ())), preferred_element_type=F32)


def at(base, size):
    return pl.ds(pl.multiple_of(base, size), size)


def halves(row):
    hi = row.astype(BF16).astype(F32)
    return hi, row - hi


def stat_rows(rows, lanes):
    place = lax.broadcasted_iota(jnp.int32, (16, lanes), 0)
    out = jnp.zeros((16, lanes), F32)
    for i, row in enumerate(rows):
        hi, lo = halves(row)
        out = jnp.where(place == 2 * i, hi, out)
        out = jnp.where(place == 2 * i + 1, lo, out)
    return out.astype(BF16)


def read_stat(ref, start, count, lane=0):
    block = ref[start : start + 16, lane:].astype(F32)
    return [block[2 * i : 2 * i + 1] + block[2 * i + 1 : 2 * i + 2] for i in range(count)]


def lane_sums(values):
    part = values[:, :128]
    for j in range(1, values.shape[1] // 128):
        part = part + values[:, j * 128 : (j + 1) * 128]
    return [
        jnp.sum(part[i * 128 : (i + 1) * 128].T, axis=0, keepdims=True)
        for i in range(values.shape[0] // 128)
    ]


def columns(rows):
    return jnp.concatenate([jnp.broadcast_to(r, (128, 128)).T for r in rows], axis=0)


def swap_pairs(v):
    even = lax.broadcasted_iota(jnp.int32, v.shape, 1) % 2 == 0
    return jnp.where(even, pltpu.roll(v, 127, 1), pltpu.roll(v, 1, 1))


def token_of(x, zl, spot):
    there = (x - (spot // 128) % 4) & 3
    return there * 256 + (zl ^ ((spot // 64) & 1)) * 128 + (spot // 512) * 64 + (spot & 63)


def k_prep(cotangent, mask, segments, ct, begin, cos, sin, cos_k, sin_k):
    y, _, x, zl, c = place()
    m = mask[...].astype(F32)
    column = jnp.broadcast_to(jnp.concatenate([m, m], axis=1), (128, 128)).T[0:64]
    for j in range(4):
        lanes = slice(j * 128, (j + 1) * 128)
        ct[0:64, lanes] = jnp.where(column > 0, cotangent[:, lanes].astype(F32), 0.0).astype(BF16)
    count = jnp.sum(m, axis=1, keepdims=True)
    ct[64:80, :] = jnp.broadcast_to(count, (16, 512)).astype(BF16)
    for s in (1, 2, 3):
        below = jnp.where(segments[...] < s, 1.0, 0.0)
        total = jnp.sum(jnp.sum(below, axis=0, keepdims=True), axis=1, keepdims=True)
        begin[s : s + 1, :] = jnp.broadcast_to(total, (1, 128))
    lane = lax.broadcasted_iota(jnp.int32, (1, 128), 1)
    rate = jnp.exp((lane // 2).astype(F32) * (-2.0 * math.log(rope_theta) / DH))
    spot = lax.broadcasted_iota(jnp.int32, (256, 1), 0) + y * 256
    angle = token_of(x, zl, spot).astype(F32) * rate
    co, si = jnp.cos(angle), jnp.sin(angle)
    si = jnp.where(lane % 2 == 0, -si, si)
    cos[...] = co
    sin[...] = si
    cos_k[...] = jnp.where(lane < 64, jnp.where(c == 0, co, pltpu.roll(co, 64, 1)), 1.0)
    sin_k[...] = jnp.where(lane < 64, jnp.where(c == 0, si, pltpu.roll(si, 64, 1)), 0.0)


def k_proj(mine, other, gain, wq, wk, wv, wkv, x_full, xg_full, *outs):
    y, _, _, _, c = place()
    wkv[0:64, :] = wk[...]
    wkv[64:128, :] = wv[...]
    x_full[at(c * 512, 512), :] = mine[...]
    x_full[at((1 - c) * 512, 512), :] = other[...]
    for k, (kv, q) in enumerate(zip(outs[:4], outs[4:])):
        rows = at(((y + k) & 3) * 256, 256)
        xf = x_full[rows, :].astype(F32)
        xg, rest = split(xf * gain[...])
        xg_full[rows, :] = xg
        sums = lane_sums(xf * xf)
        q[...] = (dot(xg, wq[...]) + dot(rest, wq[...])).astype(q.dtype)
        kv[0:256, :] = (dot(xg, wkv[...], 1, 1) + dot(rest, wkv[...], 1, 1)).astype(kv.dtype)
        if k == 0:
            kv[256:257, :] = sums[0]
            kv[257:258, :] = sums[1]
        else:
            kv[256:272, :] = stat_rows(sums, 128)


def split(v):
    hi = v.astype(BF16)
    return hi, (v - hi.astype(F32)).astype(BF16)


def k_ct(mine, other, w, full, own, m1, m2, m3, cscale):
    y, _, _, _, c = place()
    count = jnp.zeros((16, 512), F32)
    for ref, base in ((mine, c * 512), (other, (1 - c) * 512)):
        for j in range(8):
            full[at(base + j * 64, 64), :] = ref[j * 80 : j * 80 + 64, :]
            count = count + ref[j * 80 + 64 : j * 80 + 80, :].astype(F32)
    cscale[...] = TOKENS / count[0:8, 0:128]
    for k, out in enumerate((own, m1, m2, m3)):
        out[...] = dot(full[at(((y + k) & 3) * 256, 256), :], w[...]).astype(out.dtype)


def k_sum_kv(own, *refs):
    *got, out, kept = refs
    total = own[0:256, :] + sum(r[0:256, :].astype(F32) for r in got)
    stats = [read_stat(r, 256, 2) for r in got]
    sums = [own[256 + i : 257 + i, :] + sum(s[i] for s in stats) for i in range(2)]
    write_kv(total, sums, out, kept)


def write_kv(total, sums, out, kept):
    kept[0:256, :] = total
    kept[256:257, :] = sums[0]
    kept[257:258, :] = sums[1]
    out[0:256, :] = total.astype(BF16)
    out[256:272, :] = stat_rows(sums, 128)


def k_sum_heads(p0, p1, p2, p3, d0, d1, d2, d3, *outs):
    zh = place()[1]
    for k, out in enumerate(outs):
        lanes = at(((zh + k) & 3) * 128, 128)
        out[:, 0:128] = sum(r[:, lanes].astype(F32) for r in (p0, p1, p2, p3)).astype(out.dtype)
        out[:, 128:256] = sum(r[:, lanes].astype(F32) for r in (d0, d1, d2, d3)).astype(out.dtype)


def k_kv(own, got, cos, sin, kv, proj, rstd):
    stats = read_stat(got, 256, 2)
    sums = [own[256 + i : 257 + i, :] + stats[i] for i in range(2)]
    scale = columns([lax.rsqrt(s / WIDTH + norm_eps) for s in sums])
    p = own[0:256, :] + got[0:256, :].astype(F32)
    proj[...] = p
    rstd[...] = scale
    v = p * scale
    kv[...] = (v * cos[...] + swap_pairs(v) * sin[...]).astype(BF16)


def k_attend(
    p0, p1, p2, p3, cscale, rstd, cos, sin, kvm, kvo, begins, out, keep, send
):
    scale = DH ** (-0.5)
    y, _, x, zl, c = place()
    sums = sum(r[...].astype(F32) for r in (p0, p1, p2, p3))
    proj = sums[:, 0:128]
    qv = proj * rstd[...]
    q = (qv * cos[...] + swap_pairs(qv) * sin[...]).astype(BF16)
    grad = (sums[:, 128:256] * cscale[0:1, :]).astype(BF16)
    mine, other = kvm[...].astype(F32), kvo[...].astype(F32)
    first = c == 0
    lo, hi = jnp.where(first, mine, other), jnp.where(first, other, mine)
    left = lax.broadcasted_iota(jnp.int32, (TOKENS, 128), 1) < 64
    keys = jnp.where(left, lo, pltpu.roll(hi, 64, 1)).astype(BF16)
    values = jnp.where(left, pltpu.roll(lo, 64, 1), hi).astype(BF16)
    t = token_of(x, zl, lax.broadcasted_iota(jnp.int32, (256, 1), 0) + y * 256)
    start = jnp.zeros((256, 1), jnp.int32)
    for s in (1, 2, 3):
        begin = begins[s : s + 1, 0:1].astype(jnp.int32)
        start = jnp.where(t >= begin, jnp.maximum(start, begin), start)
    spot = lax.broadcasted_iota(jnp.int32, (1, TOKENS), 1)
    u = token_of(x, zl, ((y - spot // 256) & 3) * 256 + (spot & 255))
    allowed = (u <= t) & (u >= start)
    scores = jnp.where(allowed, dot(q, keys, 1, 1) * scale, -jnp.inf)
    top = jnp.max(scores, axis=1, keepdims=True)
    e = jnp.exp(scores - top)
    probs = e * (1.0 / jnp.sum(e, axis=1, keepdims=True))
    pb = probs.astype(BF16)
    attended = dot(pb, values).astype(BF16)
    out[272:528, :] = attended
    delta = jnp.sum(grad.astype(F32) * attended.astype(F32), axis=1, keepdims=True)
    ds = (probs * (dot(grad, values, 1, 1) - delta)).astype(BF16)
    dq = dot(ds, keys) * scale
    e_q = ((dq * cos[...] - swap_pairs(dq) * sin[...]) * rstd[...]).astype(BF16)
    out[0:256, :] = e_q
    out[256:272, :] = stat_rows(lane_sums(e_q.astype(F32) * proj), 128)
    dk = dot(ds, q, 0, 0) * scale
    dv = dot(pb, grad, 0, 0)
    g_lo = jnp.where(left, dk, pltpu.roll(dv, 64, 1))
    g_hi = jnp.where(left, pltpu.roll(dk, 64, 1), dv)
    keep[...] = jnp.where(first, g_lo, g_hi)
    send[...] = jnp.where(first, g_hi, g_lo).astype(BF16)


def k_dkv_core(keep, got, own, m1, m2, m3):
    for k, out in enumerate((own, m1, m2, m3)):
        rows = slice(k * 256, (k + 1) * 256)
        out[...] = (keep[rows, :] + got[rows, :].astype(F32)).astype(out.dtype)


def k_dkv_sum(own, *refs):
    *got, out, kept = refs
    total = own[...] + sum(r[...].astype(F32) for r in got)
    kept[...] = total
    out[...] = total.astype(BF16)


def k_dkv(own, got, cos, sin, rstd, proj, out):
    g = own[...] + got[...].astype(F32)
    e = ((g * cos[...] - swap_pairs(g) * sin[...]) * rstd[...]).astype(BF16)
    out[0:256, :] = e
    rows = lane_sums(e.astype(F32) * proj[...])
    scales = [rstd[i * 128 : (i + 1) * 128, :].T[0:1, :] for i in range(2)]
    out[256:272, :] = stat_rows(rows + scales, 128)


def k_pack_heads(a, b, cd, out):
    zh = place()[1]
    for head, r, row in ((zh, a, 0), (zh ^ 1, b, 0), (zh ^ 3, cd, 0), (zh ^ 2, cd, 272)):
        out[0:256, at(head * 128, 128)] = r[row : row + 256, :]
    stats = [read_stat(r, 256 + row, 2) for r, row in ((a, 0), (b, 0), (cd, 0), (cd, 272))]
    block = stat_rows([sum(s[i] for s in stats) for i in range(2)], 128)
    for k in range(4):
        out[256:272, k * 128 : (k + 1) * 128] = block


def k_pack_att(a, b, cd, out):
    zh = place()[1]
    for head, r, row in ((zh, a, 272), (zh ^ 1, b, 272), (zh ^ 3, cd, 0), (zh ^ 2, cd, 256)):
        out[:, at(head * 128, 128)] = r[row : row + 256, :]


def k_dnorm(
    q0, q1, q2, q3, k0, k1, k2, k3, wq, wkv, x_full, send, keep, keep_stat, rstd, grad, nsum, rsum
):
    y, _, _, _, c = place()
    gain = jnp.zeros((1, 512), F32)
    for k, (q, kv) in enumerate(((q0, k0), (q1, k1), (q2, k2), (q3, k3))):
        block = (y - k) & 3
        rows = at(block * 256, 256)
        g = dot(q[0:256, :], wq[...], 1, 1) + dot(kv[0:256, :], wkv[...])
        grad[rows, :] = g
        gain = gain + jnp.sum(g * x_full[rows, :].astype(F32), axis=0, keepdims=True)
        nq = read_stat(q, 256, 2)
        nk = read_stat(kv, 256, 4)
        for i in range(2):
            lanes = slice(i * 128, (i + 1) * 128)
            nsum[block, :, lanes] = jnp.broadcast_to(nq[i][:, :128] + nk[i], (8, 128))
            rsum[block, :, lanes] = jnp.broadcast_to(nk[2 + i], (8, 128))
    n = [jnp.concatenate([nsum[2 * h, 0:1, :], nsum[2 * h + 1, 0:1, :]], axis=1) for h in (c, 1 - c)]
    there = at((1 - c) * 512, 512)
    here = at(c * 512, 512)
    send[0:512, :] = grad[there, :].astype(BF16)
    send[512:528, :] = stat_rows([gain, n[1]], 512)
    keep[...] = grad[here, :]
    keep_stat[0:1, :] = gain
    keep_stat[1:2, :] = n[0]
    rstd[...] = rsum[2 * c, :, 0:128]


def k_g_core(keep, keep_stat, got, m0, m1, m2, m3):
    gain, n = read_stat(got, 512, 2)
    gain = gain + keep_stat[0:1, :]
    n = n + keep_stat[1:2, :]
    for k, out in enumerate((m0, m1, m2, m3)):
        rows = slice(k * 128, (k + 1) * 128)
        out[0:128, :] = (keep[rows, :] + got[rows, :].astype(F32)).astype(BF16)
        part = jnp.concatenate([n[:, k * 128 : (k + 1) * 128], jnp.zeros((1, 384), F32)], axis=1)
        out[128:144, :] = stat_rows([gain, part], 512)


def k_g_x(a, b, c, d, keep, send):
    refs = (a, b, c, d)
    stats = [read_stat(r, 128, 2) for r in refs]
    gain, n = (sum(s[i] for s in stats) for i in range(2))
    total = sum(r[0:128, :].astype(F32) for r in refs)
    keep[0:64, :] = total[0:64]
    keep[64:65, :] = gain
    keep[65:66, :] = n
    send[0:64, :] = total[64:128].astype(BF16)
    n_there = jnp.concatenate([n[:, 64:128], n[:, 0:64], n[:, 128:512]], axis=1)
    send[64:80, :] = stat_rows([gain, n_there], 512)


def k_final(keep, got, x, ct, gain_in, cscale, rstd, res, gain, inner):
    stats = read_stat(got, 64, 2)
    gain[...] = keep[64:65, :] + stats[0]
    n = (keep[65:66, :] + stats[1])[:, 0:128]
    inner[...] = n[:, 0:64]
    scale = rstd[0:1, :]
    corr = columns([scale * scale * n * (1.0 / WIDTH)])[0:64]
    g = keep[0:64, :] + got[0:64, :].astype(F32)
    for j in range(4):
        lanes = slice(j * 128, (j + 1) * 128)
        scaled = (ct[0:64, lanes].astype(F32) * cscale[0:1, :]).astype(BF16).astype(F32)
        res[:, lanes] = (
            scaled + g[:, lanes] * gain_in[:, lanes] - x[:, lanes].astype(F32) * corr
        ).astype(BF16)


def k_grad_w(xg_full, q0, q1, q2, q3, k0, k1, k2, k3, gq, gk, gv):
    y = place()[0]
    gkv = jnp.zeros((128, 512), F32)
    for k, (q, kv) in enumerate(((q0, k0), (q1, k1), (q2, k2), (q3, k3))):
        left = xg_full[at(((y - k) & 3) * 256, 256), :]
        part = dot(left, q[0:256, :], 0, 0)
        gq[...] = part if k == 0 else gq[...] + part
        gkv = gkv + dot(kv[0:256, :], left, 0, 0)
    gk[...] = gkv[0:64]
    gv[...] = gkv[64:128]


def k_grad_o(ct_full, a, b, c, d, cscale, go):
    y = place()[0]
    for k, r in enumerate((a, b, c, d)):
        part = dot(ct_full[at(((y - k) & 3) * 256, 256), :], r[...], 0, 0)
        go[...] = part if k == 0 else go[...] + part
    go[...] = go[...] * cscale[0:1, 0:1]


def shards(hidden, gain, wq, wk, wv, wo, cotangent, mask, segments):
    gain2 = gain[None, :]
    order = Order()
    table = ((256, 128), F32)

    x_got = shift(hidden, "zl")
    ct0, begin, cos_q, sin_q, cos_k, sin_k = call(
        k_prep,
        [((80, 512), BF16), ((8, 128), F32)] + [table] * 4,
        cotangent, mask[None, :], segments.reshape(8, 128),
    )
    ct_got = shift(ct0, "zl")
    xs = jnp.concatenate([hidden, order.after(x_got, ct0)], axis=0)
    x_parts = spread([xs] * 4, "x")
    x_parts[0] = order.after(x_parts[0], ct_got)
    x_mine = jnp.concatenate([xs, *x_parts], axis=0)
    x_other = shift(x_mine, "c")
    cs = jnp.concatenate([ct0, order.after(ct_got, *x_parts)], axis=0)
    ct_parts = spread([cs] * 4, "x")

    message = ((272, 128), BF16)
    own_kv = ((264, 128), F32)
    wkv, x_full, xg_full, kv_own, *parts = call(
        k_proj,
        [((128, 512), BF16)]
        + [((1024, 512), BF16)] * 2
        + [own_kv] + [message] * 3
        + [((256, 512), F32)] + [((256, 512), BF16)] * 3,
        x_mine, x_other, gain2, wq, wk.T, wv.T,
    )
    kv_got = spread([None, *parts[:3]], "y")
    p_own, *p_part = parts[3:]
    p_got = spread([None, *[order.after(part, *kv_got) for part in p_part]], "y")
    ct_mine = jnp.concatenate([cs, *[order.after(part, *kv_got) for part in ct_parts]], axis=0)
    ct_other = shift(ct_mine, "c")
    ct_full, d_own, d1, d2, d3, cscale = call(
        k_ct,
        [((1024, 512), BF16), ((256, 512), F32)] + [((256, 512), BF16)] * 3 + [((8, 128), F32)],
        ct_mine, ct_other, wo,
    )
    kv_sum, kv_kept = call(k_sum_kv, [message, own_kv], kv_own, *kv_got)
    kv_next = pair(kv_sum, "zh", 1)
    d_got = spread([None] + [order.after(part, kv_next) for part in (d1, d2, d3)], "y")
    kv_sum, kv_kept = call(
        k_sum_kv, [message, own_kv], order.after(kv_kept, d1), kv_next
    )
    kv_next = pair(kv_sum, "zh", 3)
    heads = call(
        k_sum_heads,
        [((256, 256), F32)] + [((256, 256), BF16)] * 3,
        p_own, *p_got, d_own, *d_got,
    )
    heads = [heads[0], *spread(heads, "zh", 1, (2, 1, 3))]
    kv, proj_kv, rstd = call(
        k_kv, [((256, 128), BF16), table, table], kv_kept, kv_next, cos_k, sin_k
    )
    kv_parts = spread([kv] * 4, "y")
    kv_parts[0] = order.after(kv_parts[0], *heads[1:])
    kv_mine = jnp.concatenate([kv, *kv_parts], axis=0)
    kv_other = shift(kv_mine, "c")

    eq, keep, send = call(
        k_attend,
        [((528, 128), BF16), ((1024, 128), F32), ((1024, 128), BF16)],
        *heads, cscale, rstd, cos_q, sin_q, kv_mine, kv_other, begin,
        unread=order.take(),
    )
    dkv_own, *dkv = call(k_dkv_core, [table] + [((256, 128), BF16)] * 3, keep, shift(send, "c"))
    dkv_got = spread([None, *dkv], "y", -1, (2, 1, 3))
    eq_next = order.after(pair(eq, "zh", 1), *dkv_got)
    eq_two = pair(jnp.concatenate([eq[:272], eq_next[:272]], axis=0), "zh", 3)
    small = [((256, 128), BF16), table]
    dkv_sum, dkv_kept = call(k_dkv_sum, small, dkv_own, *dkv_got)
    dkv_next = pair(dkv_sum, "zh", 1)
    (eq_row,) = call(k_pack_heads, [((272, 512), BF16)], eq, eq_next, eq_two)
    eq_rows = [eq_row, *spread([eq_row] * 4, "y")]
    dkv_sum, dkv_kept = call(k_dkv_sum, small, dkv_kept, dkv_next)
    dkv_next = pair(dkv_sum, "zh", 3)
    att_cat = jnp.concatenate([eq[272:], eq_next[272:]], axis=0)
    att_two = pair(order.after(att_cat, dkv_sum), "zh", 3)
    (ekv,) = call(k_dkv, [message], dkv_kept, dkv_next, cos_k, sin_k, rstd, proj_kv)
    ekv_rows = [ekv, *spread([ekv] * 4, "y")]

    ekv_rows[1] = order.after(ekv_rows[1], att_two)
    send_g, keep_g, keep_stat, rstd_col = call(
        k_dnorm,
        [((528, 512), BF16), ((512, 512), F32), ((8, 512), F32), ((8, 128), F32)],
        *eq_rows, *ekv_rows, wq, wkv, x_full,
        scratch=[
            pltpu.VMEM((1024, 512), F32),
            pltpu.VMEM((4, 8, 256), F32),
            pltpu.VMEM((4, 8, 256), F32),
        ],
        unread=order.take(),
    )
    (att_row,) = call(k_pack_att, [((256, 512), BF16)], eq, eq_next, order.after(att_two, *ekv_rows))
    att_rows = [att_row, *spread([att_row] * 4, "y")]
    got_g = shift(send_g, "c")
    g_parts = call(k_g_core, [((144, 512), BF16)] * 4, keep_g, keep_stat, got_g)
    g_got = spread(g_parts, "x", -1, (2, 1, 3))
    gq, gk, gv = call(
        k_grad_w,
        [((512, 512), F32), ((64, 512), F32), ((64, 512), F32)],
        xg_full, *eq_rows, *ekv_rows,
    )
    keep_z, send_z = call(k_g_x, [((72, 512), F32), ((80, 512), BF16)], g_parts[0], *g_got)
    got_z = shift(send_z, "zl")
    (go,) = call(k_grad_o, [((512, 512), F32)], ct_full, *att_rows, cscale)
    res, gain_grad, inner = call(
        k_final,
        [((64, 512), BF16), ((1, 512), F32), ((1, 64), F32)],
        keep_z, got_z, hidden, ct0, gain2, cscale, rstd_col,
        unread=order.take(),
    )
    return res, gain_grad[0], gq, gk.T, gv.T, go, inner[0]


def solution(mesh):
    return jax.shard_map(
        shards,
        mesh=mesh,
        in_specs=(
            P("col", "row"),
            P("row"),
            P("row", "col"),
            P("row", "col"),
            P("row", "col"),
            P("row", "col"),
            P("col", "row"),
            P("col"),
            P(),
        ),
        out_specs=(
            P("col", "row"),
            P("row"),
            P("row", "col"),
            P("row", "col"),
            P("row", "col"),
            P("row", "col"),
            P("col"),
        ),
        check_vma=False,
    )
```
